256 devices in a mesh: seq: 32 (over z, x), exp: 8 (over y, core).
Axes of the slice: x: 4, y: 4, z: 8, core: 2. Of those that a mesh axis runs over, the one named last changes fastest.
Arguments:
- x_resid: bfloat16 [16384, 2048], P(('seq', 'exp')), may hold values from -36 to 36
- queries: bfloat16 [16384, 2048], P('seq', 'exp'), may hold values from -6 to 6
- key_proj: bfloat16 [16384, 2048], P('seq', 'exp'), may hold values from -6 to 6
- val_proj: bfloat16 [16384, 2048], P('seq', 'exp'), may hold values from -6 to 6
- w_out: bfloat16 [2048, 2048], P('exp'), may hold values from -0.125 to 0.125
- norm_gain: float32 [2048], replicated, may hold values from 0.1 to 1.9
- w_gate: bfloat16 [8, 2048, 1408], P('exp', 'seq'), may hold values from -0.125 to 0.125
- w_up: bfloat16 [8, 2048, 1408], P('exp', 'seq'), may hold values from -0.125 to 0.125
- w_down: bfloat16 [8, 1408, 2048], P('exp', None, 'seq'), may hold values from -0.15625 to 0.15625
- routes: int32 [16384, 2], P(('seq', 'exp')), may hold values from 0 to 7, all different within a row; in each aligned block of 64 rows (0 to 63, 64 to 127, ...) at most 18 rows name the same one
- gate_prob: float32 [16384, 2], P(('seq', 'exp')), may hold values from 0.05 to 0.6
- grad_out: bfloat16 [16384, 2048], P(('seq', 'exp')), may hold values from -6 to 6
Outputs:
- layer_out: bfloat16 [16384, 2048], P(('seq', 'exp'))
- grad_in: bfloat16 [16384, 2048], P(('seq', 'exp'))
- grad_gate: float32 [16384, 2], P(('seq', 'exp'))
The draws below stay inside these ranges and needn't reach their ends.
Inputs may be any that keep to these rules, and one draw needn't show every extreme that they name: `routes`: in each aligned block of 64 tokens (the tokens of one device) no expert is named by more than 18 rows, a bound that some block reaches; a token's two experts differ.
All inputs are finite; a program needn't handle non-finite values.
Results may differ from the reference program's by a relative error of at most 0.024.
Values may be sent and summed in bfloat16 or wider, within the bound.
No kernel may reach another device: no remote copies, remote signals or barrier semaphores. Data moves between devices by JAX's collectives and lax.ppermute only.
A program may use at most 128 MiB of HBM per device.

```python
import math
import jax
import jax.numpy as jnp
import numpy as np
from jax import lax

D = 2048
H = 1408
HEADS = 16
HD = 128
W = 2048
TOK_SEQ = 512
TOKENS = 16384
TOK_DEV = 64
EXPERTS = 8
CAP = 18
GROUP_HEADS = 2
N_EXP = 8


def draw_x_resid(key, part):
    col_scale = jnp.exp(jax.random.uniform(jax.random.fold_in(key, 4), (1, D), jnp.float32, math.log(0.3), math.log(3.0)))
    row_scale = jnp.exp(jax.random.uniform(jax.random.fold_in(key, 3), (TOKENS, 1), jnp.float32, math.log(0.3), math.log(3.0)))
    base = jnp.clip(jax.random.normal(jax.random.fold_in(key, 5), (TOKENS, D), jnp.float32), -4.0, 4.0)
    return (base * row_scale * col_scale).astype(jnp.bfloat16)


def draw_queries(key, part):
    base = jnp.clip(1.5 * jax.random.normal(jax.random.fold_in(key, 1), (TOKENS, HEADS * HD), jnp.float32), -6.0, 6.0)
    return base.astype(jnp.bfloat16)


def draw_key_proj(key, part):
    base = jnp.clip(1.5 * jax.random.normal(jax.random.fold_in(key, 2), (TOKENS, HEADS * HD), jnp.float32), -6.0, 6.0)
    return base.astype(jnp.bfloat16)


def levels(stream_key, dims, shards, least, largest):
    def one(axis_at, shards_of):
        steps = jax.random.uniform(jax.random.fold_in(jax.random.fold_in(stream_key, 6), axis_at), (shards_of,), jnp.float32, least / len(shards), largest / len(shards))
        return jnp.repeat(jnp.exp(steps), dims[axis_at] // shards_of).reshape((-1,) + (1,) * (len(dims) - axis_at - 1))

    factor_of = one(*shards[0])
    for cut in shards[1:]:
        factor_of = factor_of * one(*cut)
    return factor_of


def shared_out(own_key, own, number, rows, number_of, top, limit, skew):
    sequence = jax.random.permutation(own_key, number_of)
    heavy_load, usual = load_shares(number_of, rows * top, limit, skew, True), load_shares(number_of, rows * top, limit, skew, False)
    places = jnp.arange(number_of)

    def named(tallies, offset_by):
        used = int((tallies > 0).sum())
        fixed = max(1, used // 4)
        shifted = fixed + (places - fixed + offset_by * (used - fixed)) % max(1, number_of - fixed)
        return jnp.zeros((number_of,), jnp.int32).at[sequence[jnp.where(places < fixed, places, shifted)]].set(jnp.asarray(tallies, jnp.int32))

    tallies = jnp.where(number % 4 == 0, named(heavy_load, number // 4), named(usual, number - number // 4 - 1))
    mixed = jax.random.permutation(jax.random.fold_in(own, 3), number_of)
    source_of, sink = mixed[0:number_of // 2 * 2:2], mixed[1:number_of // 2 * 2:2]
    room = jnp.minimum(tallies[source_of] - 1, limit - tallies[sink]) // 2
    room = jnp.where((source_of == sequence[0]) | (sink == sequence[0]) | (tallies[sink] == 0), 0, jnp.maximum(room, 0))
    shifted = jax.random.randint(jax.random.fold_in(own, 4), (number_of // 2,), 0, 1 << 20) % (room + 1)
    tallies = tallies.at[source_of].add(-shifted).at[sink].add(shifted)
    labels = jnp.searchsorted(jnp.cumsum(tallies), jnp.arange(rows * top), side="right").astype(jnp.int32)
    table = labels.reshape(top, rows).T
    table = table[jax.random.permutation(jax.random.fold_in(own, 1), rows)]
    offset_by = jax.random.randint(jax.random.fold_in(own, 2), (rows, 1), 0, top)
    return jnp.take_along_axis(table, (jnp.arange(top)[None, :] + offset_by) % top, axis=1)


def load_shares(amount, total, limit, skew, full):
    loads = [(1 << 20) // math.isqrt(standing ** skew) + 1 for standing in range(1, amount + 1)]
    largest = limit if full else min(limit, max(-(-total // amount), total * loads[0] // sum(loads)))
    least = 1 if total - largest >= amount - 1 else 0
    holding, spare = [largest] + [least] * (amount - 1), total - largest - least * (amount - 1)
    while spare > 0:
        candidates = [i for i in range(1, amount) if holding[i] < largest] or [i for i in range(1, amount) if holding[i] < limit]
        pool, left = sum([loads[i] for i in candidates]), spare
        for i in candidates:
            extra = min(limit - holding[i], max(1, left * loads[i] // pool), spare)
            holding[i] = holding[i] + extra
            spare = spare - extra
    return np.array(holding)


def noise(rng, extent, scale, limit, pieces=(), kind=jnp.bfloat16):
    loudness = levels(rng, extent, pieces, -0.22, 0.18) if pieces else 1.0
    entries = jax.random.normal(rng, extent, jnp.float32) * scale * loudness
    return jnp.minimum(jnp.maximum(entries, -limit), limit).astype(kind)


def setup_inputs(seed: int = 0) -> dict:
    splits = jax.random.split(jax.random.key(seed), 13)
    x_resid = draw_x_resid(jax.random.fold_in(splits[12], 71), 0)
    queries = draw_queries(jax.random.fold_in(splits[12], 71), 0)
    key_proj = draw_key_proj(jax.random.fold_in(splits[12], 71), 0)
    val_proj = noise(splits[3], (TOKENS, HEADS * HD), 1.0, 6.0, ((0, 32), (1, 8)))
    w_out = noise(splits[4], (HEADS * HD, D), (HEADS * HD) ** -0.5, 0.125, ((0, 8),))
    norm_gain = jnp.clip(1.0 + 0.18 * jax.random.normal(splits[5], (D,), jnp.float32), 0.1, 1.9)
    w_gate = noise(splits[6], (EXPERTS, D, H), D ** -0.5, 0.125, ((0, 8), (1, 32)))
    w_up = noise(splits[7], (EXPERTS, D, H), D ** -0.5, 0.125, ((0, 8), (1, 32)))
    w_down = noise(splits[8], (EXPERTS, H, D), H ** -0.5, 0.15625, ((0, 8), (2, 32)))
    routes_keys = jax.random.split(jax.random.fold_in(splits[9], 1), TOKENS // TOK_DEV)
    routes_turns = jax.random.permutation(jax.random.fold_in(splits[9], 3), TOKENS // TOK_DEV)
    routes = jax.vmap(lambda own, number: shared_out(jax.random.fold_in(splits[9], 2), own, number, TOK_DEV, EXPERTS, 2, CAP, 2))(routes_keys, routes_turns).reshape((TOKENS, 2))
    gate_prob = jnp.clip(0.05 + 0.55 * jax.random.uniform(splits[10], (TOKENS, 2), jnp.float32) ** levels(splits[10], (TOKENS, 2), ((0, 256),), -0.2, 0.2), 0.05, 0.6)
    grad_out = noise(splits[11], (TOKENS, D), 1.0, 6.0, ((0, 256),))
    return dict(x_resid=x_resid, queries=queries, key_proj=key_proj, val_proj=val_proj, w_out=w_out, norm_gain=norm_gain, w_gate=w_gate, w_up=w_up, w_down=w_down, routes=routes, gate_prob=gate_prob, grad_out=grad_out)


norm_eps = 1e-06

def reference(x_resid, queries, key_proj, val_proj, w_out, norm_gain, w_gate, w_up, w_down, routes, gate_prob, grad_out):
    feat_width = HEADS * HD
    score_scale = 1.0 / math.sqrt(HD)
    zero_front = jnp.zeros((W, feat_width), jnp.bfloat16)
    key_padded = jnp.concatenate([zero_front, key_proj], axis=0)
    val_padded = jnp.concatenate([zero_front, val_proj], axis=0)

    def block_attention(block_idx):
        row_start = block_idx * TOK_SEQ
        query_heads = lax.dynamic_slice_in_dim(queries, row_start, TOK_SEQ, 0).astype(jnp.float32).reshape(TOK_SEQ, HEADS, HD)
        key_heads = lax.dynamic_slice_in_dim(key_padded, row_start, TOK_SEQ + W, 0).astype(jnp.float32).reshape(TOK_SEQ + W, HEADS, HD)
        val_heads = lax.dynamic_slice_in_dim(val_padded, row_start, TOK_SEQ + W, 0).astype(jnp.float32).reshape(TOK_SEQ + W, HEADS, HD)
        scores = jnp.einsum('qhd,khd->hqk', query_heads, key_heads) * score_scale
        query_pos = row_start + jnp.arange(TOK_SEQ, dtype=jnp.int32)
        key_pos = row_start - W + jnp.arange(TOK_SEQ + W, dtype=jnp.int32)
        offset = query_pos[:, None] - key_pos[None, :]
        allowed = (offset >= 0) & (offset < W) & (key_pos[None, :] >= 0)
        scores = jnp.where(allowed[None], scores, -jnp.inf)
        row_max = lax.optimization_barrier(jnp.max(scores, axis=-1, keepdims=True))
        exp_scores = jnp.exp(scores - row_max)
        weights = (exp_scores / lax.optimization_barrier(jnp.sum(exp_scores, axis=-1, keepdims=True))).astype(jnp.bfloat16)
        mixed_rows = jnp.einsum('hqk,khd->qhd', weights.astype(jnp.float32), val_heads)
        return mixed_rows.reshape(TOK_SEQ, feat_width).astype(jnp.bfloat16)
    attn = lax.map(block_attention, jnp.arange(TOKENS // TOK_SEQ, dtype=jnp.int32)).reshape(TOKENS, feat_width)
    group_width = GROUP_HEADS * HD
    projected = jnp.zeros((TOKENS, D), jnp.float32)
    for group_idx in range(N_EXP):
        lo_col = group_idx * group_width
        group_term = jnp.dot(attn[:, lo_col:lo_col + group_width], w_out[lo_col:lo_col + group_width], preferred_element_type=jnp.float32)
        projected = projected + lax.optimization_barrier(group_term.astype(jnp.bfloat16)).astype(jnp.float32)
    hidden_state = (x_resid.astype(jnp.float32) + projected).astype(jnp.bfloat16)
    hidden_f = hidden_state.astype(jnp.float32)
    rstd_rows = lax.rsqrt(lax.optimization_barrier(jnp.mean(hidden_f * hidden_f, axis=-1, keepdims=True)) + norm_eps)
    normed = hidden_f * rstd_rows
    moe_in = (normed * norm_gain).astype(jnp.bfloat16)
    flat_routes = routes.reshape(-1)
    row_total = 2 * TOKENS
    block_rows = 2 * TOK_DEV
    block_count = TOKENS // TOK_DEV
    one_hot = (flat_routes[:, None] == jnp.arange(EXPERTS, dtype=jnp.int32)[None, :]).astype(jnp.int32)
    one_hot = one_hot.reshape(block_count, block_rows, EXPERTS)
    before = jnp.cumsum(one_hot, axis=1) - one_hot
    slot_rank = lax.optimization_barrier(jnp.sum(before * one_hot, axis=-1)).reshape(-1)
    block_of_row = jnp.arange(row_total, dtype=jnp.int32) // block_rows
    target = block_of_row * CAP + slot_rank
    buffer_rows = block_count * CAP
    padded_in = jnp.concatenate([moe_in, jnp.zeros((1, D), jnp.bfloat16)], axis=0)
    padded_grad = jnp.concatenate([grad_out, jnp.zeros((1, D), jnp.bfloat16)], axis=0)
    row_ids = jnp.arange(row_total, dtype=jnp.int32)

    def one_expert(expert_idx):
        placed = jnp.where(flat_routes == expert_idx, target, buffer_rows)
        source = jnp.full((buffer_rows,), row_total, jnp.int32).at[placed].set(row_ids, mode='drop')
        token_idx = source // 2
        rows_in = padded_in[token_idx]
        rows_grad = padded_grad[token_idx]
        gate_mat = w_gate[expert_idx]
        up_mat = w_up[expert_idx]
        down_mat = w_down[expert_idx]
        gate_pre = jnp.dot(rows_in, gate_mat, preferred_element_type=jnp.float32)
        up_pre = jnp.dot(rows_in, up_mat, preferred_element_type=jnp.float32)
        sigma = jax.nn.sigmoid(gate_pre)
        act_vals = gate_pre * sigma
        expert_hidden = (act_vals * up_pre).astype(jnp.bfloat16)
        expert_out = jnp.dot(expert_hidden, down_mat, preferred_element_type=jnp.float32).astype(jnp.bfloat16)
        back_hidden = jnp.dot(rows_grad, down_mat.T, preferred_element_type=jnp.float32)
        grad_pre_gate = (back_hidden * up_pre * sigma * (1.0 + gate_pre * (1.0 - sigma))).astype(jnp.bfloat16)
        grad_pre_up = (back_hidden * act_vals).astype(jnp.bfloat16)
        row_grad = jnp.dot(grad_pre_gate, gate_mat.T, preferred_element_type=jnp.float32)
        row_grad = row_grad + jnp.dot(grad_pre_up, up_mat.T, preferred_element_type=jnp.float32)
        return (expert_out, row_grad.astype(jnp.bfloat16))
    out_all, grad_all = lax.map(one_expert, jnp.arange(EXPERTS, dtype=jnp.int32))
    row_out = out_all[flat_routes, target].reshape(TOKENS, 2, D).astype(jnp.float32)
    row_back = grad_all[flat_routes, target].reshape(TOKENS, 2, D).astype(jnp.float32)
    layer_out = (hidden_f + lax.optimization_barrier(jnp.sum(gate_prob[:, :, None] * row_out, axis=1))).astype(jnp.bfloat16)
    grad_gate = lax.optimization_barrier(jnp.sum(grad_out.astype(jnp.float32)[:, None, :] * row_out, axis=2))
    moe_grad = lax.optimization_barrier(jnp.sum(gate_prob[:, :, None] * row_back, axis=1))
    scaled = moe_grad * norm_gain
    grad_in = grad_out.astype(jnp.float32) + rstd_rows * (scaled - normed * lax.optimization_barrier(jnp.mean(scaled * normed, axis=-1, keepdims=True)))
    return (layer_out, grad_in.astype(jnp.bfloat16), grad_gate)
```

```python
import functools
import math

import jax
import jax.numpy as jnp
from jax import lax
from jax.experimental import pallas as pl
from jax.experimental.pallas import tpu as pltpu
from jax.sharding import PartitionSpec as P

HD = 128
W = 2048
CAP = 18
SLOT = 24
NZ = 8
NX = 4
NY = 4
norm_eps = 1e-06
F32 = jnp.float32
BF16 = jnp.bfloat16
VMEM = pl.BlockSpec(memory_space=pltpu.VMEM)
ANY = pl.BlockSpec(memory_space=pl.ANY)


def params(mib):
    return pltpu.CompilerParams(vmem_limit_bytes=mib * 2**20)


def nt(a, b):
    return lax.dot_general(a, b, (((1,), (1,)), ((), ())), preferred_element_type=F32)


def nn(a, b):
    return jnp.dot(a, b, preferred_element_type=F32)


def from_behind(block, axis, distance):
    devices = range(lax.axis_size(axis))
    route = [(i - distance, i) for i in devices if i - distance in devices]
    return lax.ppermute(block, axis, route)


def shift_y(block, d):
    return lax.ppermute(block, "exp", [(i, (i + 2 * d) % (2 * NY)) for i in range(2 * NY)])


def swap_core(block):
    return lax.ppermute(block, "exp", [(i, i ^ 1) for i in range(2 * NY)])


def window_attention(queries, key_rows, val_rows, seq_base):
    tok_seq = queries.shape[0]
    feat_width = queries.shape[1]
    head_count = feat_width // HD
    key_span = key_rows.shape[0]
    reach_len = key_span - tok_seq
    key_heads = key_rows.reshape(key_span, head_count, HD)
    val_heads = val_rows.reshape(key_span, head_count, HD)
    score_scale = 1.0 / math.sqrt(HD)
    key_pos = seq_base - reach_len + jnp.arange(key_span, dtype=jnp.int32)
    query_heads = queries.reshape(tok_seq, head_count, HD)
    scores = jnp.einsum("qhd,khd->hqk", query_heads, key_heads, preferred_element_type=F32) * score_scale
    query_pos = seq_base + jnp.arange(tok_seq, dtype=jnp.int32)
    offset = query_pos[:, None] - key_pos[None, :]
    allowed = (offset >= 0) & (offset < reach_len) & (key_pos[None, :] >= 0)
    scores = jnp.where(allowed[None], scores, -jnp.inf)
    row_max = jnp.max(scores, axis=-1, keepdims=True)
    exp_scores = jnp.exp(scores - row_max)
    weights = (exp_scores / jnp.sum(exp_scores, axis=-1, keepdims=True)).astype(BF16)
    mixed = jnp.einsum("hqk,khd->qhd", weights, val_heads, preferred_element_type=F32)
    return mixed.reshape(tok_seq, feat_width).astype(BF16)


def project_kernel(where, own, sib, w_own, w_sib, out):
    for d in range(NY):
        y = lax.rem(where[0] + d, NY)
        out[d] = (nn(own[y], w_own[...]) + nn(sib[y], w_sib[...])).astype(BF16)


def project(where, own, sib, w_own, w_sib):
    return pl.pallas_call(
        project_kernel,
        out_shape=jax.ShapeDtypeStruct((NY, own.shape[1], w_own.shape[1]), BF16),
        in_specs=[pl.BlockSpec(memory_space=pltpu.SMEM)] + [VMEM] * 4,
        out_specs=VMEM,
        compiler_params=params(24),
        cost_estimate=pl.CostEstimate(flops=2 * 256 * 512 * 2048, bytes_accessed=6 * 2**20, transcendentals=0),
    )(where, own, sib, w_own, w_sib)


def slots_of(target_rows, slots, tokens):
    at = lax.broadcasted_iota(jnp.int32, (slots, tokens), 0)
    hit = (at == target_rows[0:1, :]) | (at == target_rows[1:2, :])
    return jnp.where(hit, 1.0, 0.0).astype(BF16)


def norm_kernel(x, p0, p1, p2, p3, gain, target_rows, hidden, send):
    total = p0[...].astype(F32) + p1[...].astype(F32) + p2[...].astype(F32) + p3[...].astype(F32)
    state = (x[...].astype(F32) + total).astype(BF16)
    hidden[...] = state
    wide = state.astype(F32)
    rstd = lax.rsqrt(jnp.mean(wide * wide, axis=-1, keepdims=True) + norm_eps)
    moe_in = (wide * rstd * gain[...]).astype(BF16)
    place = slots_of(target_rows, send.shape[0], x.shape[0])
    send[...] = nn(place, moe_in).astype(BF16)


def norm_dispatch(x, parts, gain, target_rows, slots):
    tokens, width = x.shape
    return pl.pallas_call(
        norm_kernel,
        out_shape=(
            jax.ShapeDtypeStruct((tokens, width), BF16),
            jax.ShapeDtypeStruct((slots, width), BF16),
        ),
        in_specs=[VMEM] * 7,
        out_specs=(VMEM, VMEM),
        compiler_params=params(24),
        cost_estimate=pl.CostEstimate(flops=2 * slots * tokens * width, bytes_accessed=3 * 2**20, transcendentals=0),
    )(x, *parts, gain, target_rows)


def scatter_kernel(rows, target_rows, send):
    place = slots_of(target_rows, send.shape[0], rows.shape[0])
    send[...] = nn(place, rows[...]).astype(BF16)


def scatter_rows(rows, target_rows, slots):
    return pl.pallas_call(
        scatter_kernel,
        out_shape=jax.ShapeDtypeStruct((slots, rows.shape[1]), BF16),
        in_specs=[VMEM] * 2,
        out_specs=VMEM,
        compiler_params=params(16),
        cost_estimate=pl.CostEstimate(flops=2 * slots * 64 * 2048, bytes_accessed=2**20, transcendentals=0),
    )(rows, target_rows)


def expert_kernel(part, rows_in, rows_grad, chunk, out, back, wg, wu, wd, ga, ua, ba, hid, gpg, gpu, sems):
    shards = chunk.shape[0]
    mats = (wg, wu, wd)
    group = 4
    steps = shards // group
    span = group * part

    def start(s, _):
        for m in range(3):
            pltpu.make_async_copy(
                chunk.at[s, pl.ds(m * part, part)], mats[m].at[pl.ds(s * part, part)], sems.at[m, s // group]
            ).start()
        return 0

    lax.fori_loop(0, shards, start, 0)

    def wait(m, k):
        view = mats[m].at[pl.ds(k * span, span)]
        pltpu.make_async_copy(view, view, sems.at[m, k]).wait()

    for k in range(steps):
        cols = pl.ds(k * span, span)
        for m, (rows, acc) in enumerate(((rows_in, ga), (rows_in, ua), (rows_grad, ba))):
            wait(m, k)
            term = nn(rows[:, cols], mats[m][cols, :])
            acc[...] = term if k == 0 else acc[...] + term

    def point(i, _):
        r = pl.ds(pl.multiple_of(i * 16, 16), 16)
        gate, up, grad = ga[r, :], ua[r, :], ba[r, :]
        sigma = jax.nn.sigmoid(gate)
        act = gate * sigma
        hid[r, :] = (act * up).astype(BF16)
        gpg[r, :] = (grad * up * sigma * (1.0 + gate * (1.0 - sigma))).astype(BF16)
        gpu[r, :] = (grad * act).astype(BF16)
        return 0

    lax.fori_loop(0, hid.shape[0] // 16, point, 0)

    def finish(k, _):
        cols = pl.ds(pl.multiple_of(k * span, span), span)
        out[:, cols] = nt(hid[...], wd[cols, :]).astype(BF16)
        back[:, cols] = (nt(gpg[...], wg[cols, :]) + nt(gpu[...], wu[cols, :])).astype(BF16)
        return 0

    lax.fori_loop(0, steps, finish, 0)


def experts(rows_in, rows_grad, chunk):
    rows, width = rows_in.shape
    shards, depth, hidden = chunk.shape
    part = depth // 3
    made = jax.ShapeDtypeStruct((rows, width), BF16)
    return pl.pallas_call(
        functools.partial(expert_kernel, part),
        out_shape=(made, made),
        in_specs=[VMEM, VMEM, ANY],
        out_specs=(VMEM, VMEM),
        scratch_shapes=[pltpu.VMEM((width, hidden), BF16)] * 3
        + [pltpu.VMEM((rows, hidden), F32)] * 3
        + [pltpu.VMEM((rows, hidden), BF16)] * 3
        + [pltpu.SemaphoreType.DMA((3, shards // 4))],
        compiler_params=params(40),
        cost_estimate=pl.CostEstimate(
            flops=12 * rows * width * hidden, bytes_accessed=20 * 2**20, transcendentals=rows * hidden
        ),
    )(rows_in, rows_grad, chunk)


def combine_kernel(hidden, grad_out, row_out, row_back, target, prob, gain, layer_out, grad_in, grad_gate):
    tokens = hidden.shape[0]
    slots = row_out.shape[0]
    at = lax.broadcasted_iota(jnp.int32, (tokens, slots), 1)
    pick = [jnp.where(at == target[:, c : c + 1], 1.0, 0.0).astype(BF16) for c in (0, 1)]
    wide = hidden[...].astype(F32)
    grad = grad_out[...].astype(F32)
    out0, out1 = nn(pick[0], row_out[...]), nn(pick[1], row_out[...])
    p0, p1 = prob[:, 0:1], prob[:, 1:2]
    layer_out[...] = (wide + (p0 * out0 + p1 * out1)).astype(BF16)
    grad_gate[:, 0:1] = jnp.sum(grad * out0, axis=-1, keepdims=True)
    grad_gate[:, 1:2] = jnp.sum(grad * out1, axis=-1, keepdims=True)
    moe_grad = p0 * nn(pick[0], row_back[...]) + p1 * nn(pick[1], row_back[...])
    rstd = lax.rsqrt(jnp.mean(wide * wide, axis=-1, keepdims=True) + norm_eps)
    normed = wide * rstd
    scaled = moe_grad * gain[...]
    mean = jnp.mean(scaled * normed, axis=-1, keepdims=True)
    grad_in[...] = (grad + rstd * (scaled - normed * mean)).astype(BF16)


def combine(hidden, grad_out, row_out, row_back, target, prob, gain):
    tokens, width = hidden.shape
    made = jax.ShapeDtypeStruct((tokens, width), BF16)
    return pl.pallas_call(
        combine_kernel,
        out_shape=(made, made, jax.ShapeDtypeStruct((tokens, 2), F32)),
        in_specs=[VMEM] * 7,
        out_specs=(VMEM,) * 3,
        compiler_params=params(24),
        cost_estimate=pl.CostEstimate(flops=2**28, bytes_accessed=3 * 2**20, transcendentals=0),
    )(hidden, grad_out, row_out, row_back, target, prob, gain)


def per_device(
    x_resid, queries, key_proj, val_proj, w_out, norm_gain, w_gate, w_up, w_down, routes, gate_prob, grad_out
):
    tok_seq = queries.shape[0]
    tok_dev, width = x_resid.shape
    me_exp = lax.axis_index("exp")
    core, y = me_exp % 2, me_exp // 2
    stacked = jnp.concatenate([w_gate[0], w_up[0], w_down[0].T], axis=0)
    chunk = lax.all_gather(stacked, "seq", axis=0)

    flat = routes.reshape(-1)
    order = jnp.arange(flat.shape[0], dtype=jnp.int32)
    same = (flat[:, None] == flat[None, :]) & (order[None, :] < order[:, None])
    rank = jnp.sum(same.astype(jnp.int32), axis=1)
    target = (flat * SLOT + rank).reshape(tok_dev, 2)
    target_rows = target.T
    slots = 2 * NY * SLOT
    gain = norm_gain[None, :]

    def exchange(rows):
        return lax.all_to_all(
            rows.reshape(2 * NY, SLOT, width), "exp", split_axis=0, concat_axis=0, tiled=True
        ).reshape(slots, width)

    recv_grad = exchange(scatter_rows(grad_out, target_rows, slots))
    w_sib = swap_core(w_out)

    hop_count = W // tok_seq
    seq_base = lax.axis_index("seq") * tok_seq
    earlier = []
    carried = (key_proj, val_proj)
    for _ in range(hop_count):
        carried = from_behind(carried, "seq", 1)
        earlier.insert(0, carried)
    key_rows = jnp.concatenate([pair[0] for pair in earlier] + [key_proj], axis=0)
    val_rows = jnp.concatenate([pair[1] for pair in earlier] + [val_proj], axis=0)
    attn = window_attention(queries, key_rows, val_rows, seq_base)

    owners = attn.reshape(NY, 2, tok_dev, attn.shape[1])
    mine = lax.dynamic_index_in_dim(owners, core, 1, keepdims=False)
    theirs = swap_core(lax.dynamic_index_in_dim(owners, 1 - core, 1, keepdims=False))
    partial = project(y[None].astype(jnp.int32), mine, theirs, w_out, w_sib)
    parts = [partial[0]] + [shift_y(partial[d], d) for d in (1, 2, 3)]
    hidden, send_in = norm_dispatch(x_resid, parts, gain, target_rows, slots)
    recv_in = exchange(send_in)
    out_rows, back_rows = experts(recv_in, recv_grad, chunk)
    return combine(hidden, grad_out, exchange(out_rows), exchange(back_rows), target, gate_prob, gain)


def solution(mesh):
    tokens = P(("seq", "exp"), None)
    heads = P("seq", "exp")
    placed = (
        tokens,
        heads,
        heads,
        heads,
        P("exp", None),
        P(),
        P("exp", "seq", None),
        P("exp", "seq", None),
        P("exp", None, "seq"),
        tokens,
        tokens,
        tokens,
    )
    return jax.shard_map(
        per_device, mesh=mesh, in_specs=placed, out_specs=(tokens, tokens, tokens), check_vma=False
    )
```

```python
import functools
import math

import jax
import jax.numpy as jnp
from jax import lax
from jax.experimental import pallas as pl
from jax.experimental.pallas import tpu as pltpu
from jax.sharding import PartitionSpec as P

HD = 128
W = 2048
CAP = 18
SLOT = 24
BACK = 40
NZ = 8
NX = 4
NY = 4
norm_eps = 1e-06
F32 = jnp.float32
BF16 = jnp.bfloat16
VMEM = pl.BlockSpec(memory_space=pltpu.VMEM)
SMEM = pl.BlockSpec(memory_space=pltpu.SMEM)
ANY = pl.BlockSpec(memory_space=pl.ANY)


def params(mib):
    return pltpu.CompilerParams(vmem_limit_bytes=mib * 2**20)


def nt(a, b):
    return lax.dot_general(a, b, (((1,), (1,)), ((), ())), preferred_element_type=F32)


def nn(a, b):
    return jnp.dot(a, b, preferred_element_type=F32)


def shift_zx(block, dz, dx):
    route = [(s, ((s // NX + dz) % NZ) * NX + (s % NX + dx) % NX) for s in range(NZ * NX)]
    return lax.ppermute(block, "seq", route)


def along_z(block, d):
    return shift_zx(block, d, 0)


def along_x(block, d):
    return shift_zx(block, 0, d)


def along_y(block, d):
    return lax.ppermute(block, "exp", [(i, (i + 2 * d) % (2 * NY)) for i in range(2 * NY)])


def swap_core(block):
    return lax.ppermute(block, "exp", [(i, i ^ 1) for i in range(2 * NY)])


def opposite(ahead, behind, cut, move):
    return [move(ahead[:cut], 1), move(behind[cut:], -1)]


def earlier_shards(own):
    x = lax.axis_index("seq") % NX
    above = along_z(own, 1)
    one = along_x(jnp.where(x == NX - 1, above, own), 1)
    two = along_x(jnp.where(x < 2, own, above), 2)
    three = along_x(jnp.where(x == 0, own, above), -1)
    return [one, two, three, above]


def attention_kernel(where, q, k0, k1, k2, k3, k4, v0, v1, v2, v3, v4, out):
    keys, vals = (k0, k1, k2, k3, k4), (v0, v1, v2, v3, v4)
    rows, span = 128, k0.shape[0]
    scale = 1.0 / math.sqrt(HD)
    seq = where[0]

    def block(i, _):
        at = pl.multiple_of(i * rows, rows)
        qpos = at + lax.broadcasted_iota(jnp.int32, (rows, span), 0)
        kpos = lax.broadcasted_iota(jnp.int32, (rows, span), 1)
        for h in range(out.shape[1] // HD):
            cols = slice(h * HD, (h + 1) * HD)
            queries = q[pl.ds(at, rows), cols]
            scores = []
            for d in range(5):
                s = nt(queries, keys[d][:, cols]) * scale
                if d == 0:
                    s = jnp.where(kpos <= qpos, s, -jnp.inf)
                elif d == 4:
                    s = jnp.where((kpos > qpos) & (seq >= d), s, -jnp.inf)
                else:
                    s = jnp.where(seq >= d, s, -jnp.inf)
                scores.append(s)
            top = scores[0]
            for s in scores[1:]:
                top = jnp.maximum(top, s)
            top = jnp.max(top, axis=-1, keepdims=True)
            mixed = jnp.zeros((rows, HD), F32)
            total = jnp.zeros((rows, span), F32)
            for d in range(5):
                e = jnp.exp(scores[d] - top)
                total = total + e
                mixed = mixed + nn(e.astype(BF16), vals[d][:, cols])
            out[pl.ds(at, rows), cols] = (mixed / jnp.sum(total, axis=-1, keepdims=True)).astype(BF16)
        return 0

    lax.fori_loop(0, q.shape[0] // rows, block, 0)


def attention(where, q, keys, vals):
    return pl.pallas_call(
        attention_kernel,
        out_shape=jax.ShapeDtypeStruct(q.shape, BF16),
        in_specs=[SMEM] + [VMEM] * 11,
        out_specs=VMEM,
        compiler_params=params(24),
        cost_estimate=pl.CostEstimate(flops=4 * 512 * 2560 * 256, bytes_accessed=6 * 2**20, transcendentals=512 * 2560 * 2),
    )(where, q, *keys, *vals)


def gather_out(w):
    half = w.shape[0] // 2
    ahead, behind = along_y(w, 1), along_y(w, -1)
    mine = [w, ahead, behind] + opposite(ahead, behind, half, along_y)
    return mine + [swap_core(part) for part in mine]


def gather_down(rows):
    half = rows.shape[0] // 2
    quarter = half // 2
    a, b = rows[:half], rows[half:]
    ax, bx = along_x(a, 1), along_x(a, -1)
    plane = jnp.concatenate([a, ax, bx] + opposite(ax, bx, quarter, along_x), axis=0)
    runs_a = [(0, 0, half, 0), (half, 0, half, 1), (2 * half, 0, half, 3), (3 * half, 0, half, 2)]
    up, dn = [along_z(b, 1)], [along_z(b, -1)]
    for _ in range(2):
        up.append(along_z(up[-1], 1))
        dn.append(along_z(dn[-1], -1))
    column = jnp.concatenate(
        [b, up[0], dn[0], up[1], dn[1], up[2], dn[2]] + opposite(up[2], dn[2], quarter, along_z), axis=0
    )
    runs_b = [(i * half, half, half, dz) for i, dz in enumerate((0, 1, 7, 2, 6, 3, 5, 4))]
    pieces = [(plane, [(p, o, n, 0, dx) for p, o, n, dx in runs_a])]
    pieces.append((column, [(p, o, n, dz, 0) for p, o, n, dz in runs_b]))
    right, left = along_x(column, 1), along_x(column, -1)
    cut = column.shape[0] // 2
    far = opposite(right, left, cut, along_x)
    pieces.append((right, [(p, o, n, dz, 1) for p, o, n, dz in runs_b]))
    pieces.append((left, [(p, o, n, dz, 3) for p, o, n, dz in runs_b]))
    pieces.append((far[0], [(p, o, n, dz, 2) for p, o, n, dz in runs_b[:4]]))
    pieces.append((far[1], [(p - cut, o, n, dz, 2) for p, o, n, dz in runs_b[4:]]))
    ahead, behind = plane, plane
    for dz in (1, 2, 3):
        ahead, behind = along_z(ahead, 1), along_z(behind, -1)
        pieces.append((ahead, [(p, o, n, dz, dx) for p, o, n, dx in runs_a]))
        pieces.append((behind, [(p, o, n, NZ - dz, dx) for p, o, n, dx in runs_a]))
    cut = plane.shape[0] // 2
    far = opposite(ahead, behind, cut, along_z)
    pieces.append((far[0], [(p, o, n, 4, dx) for p, o, n, dx in runs_a[:2]]))
    pieces.append((far[1], [(p - cut, o, n, 4, dx) for p, o, n, dx in runs_a[2:]]))
    return [p for p, _ in pieces], [r for _, r in pieces]


def slots_of(target_rows, slots, tokens):
    at = lax.broadcasted_iota(jnp.int32, (slots, tokens), 0)
    hit = (at == target_rows[0:1, :]) | (at == target_rows[1:2, :])
    return jnp.where(hit, 1.0, 0.0).astype(BF16)


def project_kernel(where, attn, x, gain, target_rows, *refs):
    w, (hidden, send) = refs[:-2], refs[-2:]
    y, core = where[1], where[2]
    half = attn.shape[2] // 2
    total = x[...].astype(F32)
    summed = jnp.zeros(x.shape, F32)
    for flip in (0, 1):
        own, ahead, behind, first, second = w[5 * flip : 5 * flip + 5]
        c = core if flip == 0 else 1 - core
        for part, d in ((own, 0), (ahead, 3), (behind, 1)):
            summed = summed + nn(attn[lax.rem(y + d, NY) * 2 + c], part[...])
        rows = attn[lax.rem(y + 2, NY) * 2 + c]
        summed = summed + nn(rows[:, :half], first[...]) + nn(rows[:, half:], second[...])
    state = (total + summed).astype(BF16)
    hidden[...] = state
    wide = state.astype(F32)
    rstd = lax.rsqrt(jnp.mean(wide * wide, axis=-1, keepdims=True) + norm_eps)
    moe_in = (wide * rstd * gain[...]).astype(BF16)
    place = slots_of(target_rows, send.shape[0], x.shape[0])
    send[...] = nn(place, moe_in).astype(BF16)


def project_dispatch(where, attn, x, gain, target_rows, w, slots):
    tokens, width = x.shape
    return pl.pallas_call(
        project_kernel,
        out_shape=(
            jax.ShapeDtypeStruct((tokens, width), BF16),
            jax.ShapeDtypeStruct((slots, width), BF16),
        ),
        in_specs=[SMEM] + [VMEM] * (4 + len(w)),
        out_specs=(VMEM, VMEM),
        compiler_params=params(24),
        cost_estimate=pl.CostEstimate(flops=2**30, bytes_accessed=10 * 2**20, transcendentals=0),
    )(where, attn, x, gain, target_rows, *w)


def scatter_kernel(rows, target_rows, send):
    place = slots_of(target_rows, send.shape[0], rows.shape[0])
    send[...] = nn(place, rows[...]).astype(BF16)


def scatter_rows(rows, target_rows, slots):
    return pl.pallas_call(
        scatter_kernel,
        out_shape=jax.ShapeDtypeStruct((slots, rows.shape[1]), BF16),
        in_specs=[VMEM] * 2,
        out_specs=VMEM,
        compiler_params=params(16),
        cost_estimate=pl.CostEstimate(flops=2 * slots * 64 * 2048, bytes_accessed=2**20, transcendentals=0),
    )(rows, target_rows)


def expert_kernel(part, runs, where, rows_in, rows_grad, chunk, *refs):
    downs, (both, wg, wu, wd, ga, ua, ba, hid, gpg, gpu, sems, down_sem) = refs[: len(runs)], refs[len(runs) :]
    shards = chunk.shape[0]
    seq = where[0]
    z, x = seq // NX, lax.rem(seq, NX)
    mats = (wg, wu)
    group = 4
    steps = shards // group
    span = group * part

    def start(s, _):
        for m in range(2):
            pltpu.make_async_copy(
                chunk.at[s, pl.ds(m * part, part)],
                mats[m].at[pl.ds(pl.multiple_of(s * part, part), part)],
                sems.at[m, s // group],
            ).start()
        return 0

    lax.fori_loop(0, shards, start, 0)
    for piece, listed in zip(downs, runs):
        for first, offset, count, dz, dx in listed:
            source = lax.rem(z + NZ - dz, NZ) * NX + lax.rem(x + NX - dx, NX)
            row = pl.multiple_of(source * part + offset, 16)
            pltpu.make_async_copy(piece.at[pl.ds(first, count)], wd.at[pl.ds(row, count)], down_sem).start()

    for k in range(steps):
        cols = pl.ds(k * span, span)
        for m, acc in ((0, ga), (1, ua)):
            view = mats[m].at[cols]
            pltpu.make_async_copy(view, view, sems.at[m, k]).wait()
            term = nn(rows_in[:, cols], mats[m][cols, :])
            acc[...] = term if k == 0 else acc[...] + term
    pltpu.make_async_copy(wd, wd, down_sem).wait()
    for k in range(steps):
        cols = pl.ds(k * span, span)
        term = nn(rows_grad[:, cols], wd[cols, :])
        ba[...] = term if k == 0 else ba[...] + term

    def point(i, _):
        r = pl.ds(pl.multiple_of(i * 16, 16), 16)
        gate, up, grad = ga[r, :], ua[r, :], ba[r, :]
        sigma = jax.nn.sigmoid(gate)
        act = gate * sigma
        hid[r, :] = (act * up).astype(BF16)
        gpg[r, :] = (grad * up * sigma * (1.0 + gate * (1.0 - sigma))).astype(BF16)
        gpu[r, :] = (grad * act).astype(BF16)
        return 0

    lax.fori_loop(0, hid.shape[0] // 16, point, 0)
    sources = 2 * NY

    def finish(k, _):
        cols = pl.ds(pl.multiple_of(k * span, span), span)
        out = nt(hid[...], wd[cols, :]).reshape(sources, SLOT, span)
        back = (nt(gpg[...], wg[cols, :]) + nt(gpu[...], wu[cols, :])).reshape(sources, SLOT, span)
        rest = jnp.zeros((sources, BACK - 2 * CAP, span), F32)
        joined = jnp.concatenate([out[:, :CAP], back[:, :CAP], rest], axis=1)
        both[:, cols] = joined.reshape(sources * BACK, span).astype(BF16)
        return 0

    lax.fori_loop(0, steps, finish, 0)


def experts(where, rows_in, rows_grad, chunk, downs, runs):
    rows, width = rows_in.shape
    shards, depth, hidden = chunk.shape
    part = depth // 2
    return pl.pallas_call(
        functools.partial(expert_kernel, part, runs),
        out_shape=jax.ShapeDtypeStruct((2 * NY * BACK, width), BF16),
        in_specs=[SMEM, VMEM, VMEM] + [ANY] * (1 + len(downs)),
        out_specs=VMEM,
        scratch_shapes=[pltpu.VMEM((width, hidden), BF16)] * 3
        + [pltpu.VMEM((rows, hidden), F32)] * 3
        + [pltpu.VMEM((rows, hidden), BF16)] * 3
        + [pltpu.SemaphoreType.DMA((2, shards // 4)), pltpu.SemaphoreType.DMA(())],
        compiler_params=params(40),
        cost_estimate=pl.CostEstimate(
            flops=12 * rows * width * hidden, bytes_accessed=20 * 2**20, transcendentals=rows * hidden
        ),
    )(where, rows_in, rows_grad, chunk, *downs)


def combine_kernel(hidden, grad_out, rows, target, prob, gain, layer_out, grad_in, grad_gate):
    tokens = hidden.shape[0]
    at = lax.broadcasted_iota(jnp.int32, (tokens, rows.shape[0]), 1)

    def picked(c, offset):
        place = jnp.where(at == target[:, c : c + 1] + offset, 1.0, 0.0).astype(BF16)
        return nn(place, rows[...])

    wide = hidden[...].astype(F32)
    grad = grad_out[...].astype(F32)
    out0, out1 = picked(0, 0), picked(1, 0)
    p0, p1 = prob[:, 0:1], prob[:, 1:2]
    layer_out[...] = (wide + (p0 * out0 + p1 * out1)).astype(BF16)
    grad_gate[:, 0:1] = jnp.sum(grad * out0, axis=-1, keepdims=True)
    grad_gate[:, 1:2] = jnp.sum(grad * out1, axis=-1, keepdims=True)
    moe_grad = p0 * picked(0, CAP) + p1 * picked(1, CAP)
    rstd = lax.rsqrt(jnp.mean(wide * wide, axis=-1, keepdims=True) + norm_eps)
    normed = wide * rstd
    scaled = moe_grad * gain[...]
    mean = jnp.mean(scaled * normed, axis=-1, keepdims=True)
    grad_in[...] = (grad + rstd * (scaled - normed * mean)).astype(BF16)


def combine(hidden, grad_out, rows, target, prob, gain):
    tokens, width = hidden.shape
    made = jax.ShapeDtypeStruct((tokens, width), BF16)
    return pl.pallas_call(
        combine_kernel,
        out_shape=(made, made, jax.ShapeDtypeStruct((tokens, 2), F32)),
        in_specs=[VMEM] * 6,
        out_specs=(VMEM,) * 3,
        compiler_params=params(24),
        cost_estimate=pl.CostEstimate(flops=2**28, bytes_accessed=3 * 2**20, transcendentals=0),
    )(hidden, grad_out, rows, target, prob, gain)


def per_device(
    x_resid, queries, key_proj, val_proj, w_out, norm_gain, w_gate, w_up, w_down, routes, gate_prob, grad_out
):
    tok_dev, width = x_resid.shape
    me_seq, me_exp = lax.axis_index("seq"), lax.axis_index("exp")
    where = jnp.stack([me_seq, me_exp // 2, me_exp % 2]).astype(jnp.int32)
    keys = [key_proj] + earlier_shards(key_proj)
    vals = [val_proj] + earlier_shards(val_proj)
    chunk = lax.all_gather(jnp.concatenate([w_gate[0], w_up[0]], axis=0), "seq", axis=0)
    downs, runs = gather_down(w_down[0].T)
    outs = gather_out(w_out)

    flat = routes.reshape(-1)
    order = jnp.arange(flat.shape[0], dtype=jnp.int32)
    same = (flat[:, None] == flat[None, :]) & (order[None, :] < order[:, None])
    rank = jnp.sum(same.astype(jnp.int32), axis=1)
    target_rows = (flat * SLOT + rank).reshape(tok_dev, 2).T
    returned = (flat * BACK + rank).reshape(tok_dev, 2)
    sources = 2 * NY
    slots = sources * SLOT
    gain = norm_gain[None, :]

    def exchange(rows):
        split = rows.reshape(sources, rows.shape[0] // sources, rows.shape[1])
        return lax.all_to_all(split, "exp", split_axis=0, concat_axis=0, tiled=True)

    recv_grad = exchange(scatter_rows(grad_out, target_rows, slots)).reshape(slots, width)
    attn = exchange(attention(where, queries, keys, vals))
    hidden, send_in = project_dispatch(where, attn, x_resid, gain, target_rows, outs, slots)
    recv_in = exchange(send_in).reshape(slots, width)
    both = experts(where, recv_in, recv_grad, chunk, downs, runs)
    rows = exchange(both).reshape(sources * BACK, width)
    return combine(hidden, grad_out, rows, returned, gate_prob, gain)


def solution(mesh):
    tokens = P(("seq", "exp"), None)
    heads = P("seq", "exp")
    placed = (
        tokens,
        heads,
        heads,
        heads,
        P("exp", None),
        P(),
        P("exp", "seq", None),
        P("exp", "seq", None),
        P("exp", None, "seq"),
        tokens,
        tokens,
        tokens,
    )
    return jax.shard_map(
        per_device, mesh=mesh, in_specs=placed, out_specs=(tokens, tokens, tokens), check_vma=False
    )
```

```python
import functools
import math

import jax
import jax.numpy as jnp
from jax import lax
from jax.experimental import pallas as pl
from jax.experimental.pallas import tpu as pltpu
from jax.sharding import PartitionSpec as P

HD = 128
W = 2048
CAP = 18
SLOT = 24
BACK = 40
NZ = 8
NX = 4
NY = 4
norm_eps = 1e-06
F32 = jnp.float32
BF16 = jnp.bfloat16
VMEM = pl.BlockSpec(memory_space=pltpu.VMEM)
SMEM = pl.BlockSpec(memory_space=pltpu.SMEM)
HBM = pl.BlockSpec(memory_space=pltpu.HBM)


def params(mib):
    return pltpu.CompilerParams(vmem_limit_bytes=mib * 2**20)


def nt(a, b):
    return lax.dot_general(a, b, (((1,), (1,)), ((), ())), preferred_element_type=F32)


def nn(a, b):
    return jnp.dot(a, b, preferred_element_type=F32)


def shift_zx(block, dz, dx):
    route = [(s, ((s // NX + dz) % NZ) * NX + (s % NX + dx) % NX) for s in range(NZ * NX)]
    return lax.ppermute(block, "seq", route)


def along_z(block, d):
    return shift_zx(block, d, 0)


def along_x(block, d):
    return shift_zx(block, 0, d)


def along_y(block, d):
    return lax.ppermute(block, "exp", [(i, (i + 2 * d) % (2 * NY)) for i in range(2 * NY)])


def swap_core(block):
    return lax.ppermute(block, "exp", [(i, i ^ 1) for i in range(2 * NY)])


def after(value, *earlier):
    return lax.optimization_barrier((value, earlier))[0]


def opposite(ahead, behind, cut, move):
    return [move(ahead[:cut], 1), move(behind[cut:], -1)]


def to_earlier(own):
    x = lax.axis_index("seq") % NX
    above = along_z(own, 1)
    return above, (
        jnp.where(x == NX - 1, above, own),
        jnp.where(x < 2, own, above),
        jnp.where(x == 0, own, above),
    )


def earlier_shards(above, loads):
    return [along_x(loads[0], 1), along_x(loads[1], 2), along_x(loads[2], -1), above]


def attention_kernel(where, q, k0, k1, k2, k3, k4, v0, v1, v2, v3, v4, out):
    keys, vals = (k0, k1, k2, k3, k4), (v0, v1, v2, v3, v4)
    rows, span = 128, k0.shape[0]
    scale = 1.0 / math.sqrt(HD)
    seq = where[0]

    def block(i, _):
        at = pl.multiple_of(i * rows, rows)
        qpos = at + lax.broadcasted_iota(jnp.int32, (rows, span), 0)
        kpos = lax.broadcasted_iota(jnp.int32, (rows, span), 1)
        for h in range(out.shape[1] // HD):
            cols = slice(h * HD, (h + 1) * HD)
            queries = q[pl.ds(at, rows), cols]
            scores = []
            for d in range(5):
                s = nt(queries, keys[d][:, cols]) * scale
                if d == 0:
                    s = jnp.where(kpos <= qpos, s, -jnp.inf)
                elif d == 4:
                    s = jnp.where((kpos > qpos) & (seq >= d), s, -jnp.inf)
                else:
                    s = jnp.where(seq >= d, s, -jnp.inf)
                scores.append(s)
            top = scores[0]
            for s in scores[1:]:
                top = jnp.maximum(top, s)
            top = jnp.max(top, axis=-1, keepdims=True)
            mixed = jnp.zeros((rows, HD), F32)
            total = jnp.zeros((rows, span), F32)
            for d in range(5):
                e = jnp.exp(scores[d] - top)
                total = total + e
                mixed = mixed + nn(e.astype(BF16), vals[d][:, cols])
            out[pl.ds(at, rows), cols] = (mixed / jnp.sum(total, axis=-1, keepdims=True)).astype(BF16)
        return 0

    lax.fori_loop(0, q.shape[0] // rows, block, 0)


def attention(where, q, keys, vals):
    return pl.pallas_call(
        attention_kernel,
        out_shape=jax.ShapeDtypeStruct(q.shape, BF16),
        in_specs=[SMEM] + [VMEM] * 11,
        out_specs=VMEM,
        compiler_params=params(24),
        cost_estimate=pl.CostEstimate(flops=4 * 512 * 2560 * 256, bytes_accessed=6 * 2**20, transcendentals=512 * 2560 * 2),
    )(where, q, *keys, *vals)


def gather_out(w, sent):
    half = w.shape[0] // 2
    ahead, behind = along_y(w, 1), along_y(w, -1)
    mine = [w, ahead, behind] + opposite(after(ahead, sent), after(behind, sent), half, along_y)
    return mine + [swap_core(after(part, sent)) for part in mine]


def gather_rows(rows, sent, arrived):
    half = rows.shape[0] // 2
    early = 32
    a, b = rows[:half], rows[half:]
    ax, bx = along_x(a, 1), along_x(a, -1)
    up, dn = [along_z(b, 1)], [along_z(b, -1)]
    plane = jnp.concatenate([a, ax, bx] + opposite(after(ax, sent), after(bx, sent), early, along_x), axis=0)
    up.append(along_z(after(up[0], sent), 1))
    dn.append(along_z(after(dn[0], sent), -1))
    ahead, behind = [along_z(plane, 1)], [along_z(plane, -1)]
    up.append(along_z(up[1], 1))
    dn.append(along_z(dn[1], -1))
    column = jnp.concatenate(
        [b, up[0], dn[0], up[1], dn[1], up[2], dn[2]] + opposite(up[2], dn[2], early, along_z), axis=0
    )
    runs_a = [(0, 0, half, 0), (half, 0, half, 1), (2 * half, 0, half, 3), (3 * half, 0, half, 2)]
    runs_b = [(i * half, half, half, dz) for i, dz in enumerate((0, 1, 7, 2, 6, 3, 5, 4))]
    pieces = [(plane, [(p, o, n, 0, dx) for p, o, n, dx in runs_a])]
    pieces.append((column, [(p, o, n, dz, 0) for p, o, n, dz in runs_b]))
    column = after(column, arrived)
    right, left = along_x(column, 1), along_x(column, -1)
    for _ in range(2):
        ahead.append(along_z(after(ahead[-1], arrived), 1))
        behind.append(along_z(after(behind[-1], arrived), -1))
    cut = column.shape[0] // 2
    far = opposite(right, left, cut, along_x)
    pieces.append((right, [(p, o, n, dz, 1) for p, o, n, dz in runs_b]))
    pieces.append((left, [(p, o, n, dz, 3) for p, o, n, dz in runs_b]))
    pieces.append((far[0], [(p, o, n, dz, 2) for p, o, n, dz in runs_b[:4]]))
    pieces.append((far[1], [(p - cut, o, n, dz, 2) for p, o, n, dz in runs_b[4:]]))
    for i in range(3):
        pieces.append((ahead[i], [(p, o, n, 1 + i, dx) for p, o, n, dx in runs_a]))
        pieces.append((behind[i], [(p, o, n, NZ - 1 - i, dx) for p, o, n, dx in runs_a]))
    cut = plane.shape[0] // 2
    far = opposite(ahead[2], behind[2], cut, along_z)
    pieces.append((far[0], [(p, o, n, 4, dx) for p, o, n, dx in runs_a[:2]]))
    pieces.append((far[1], [(p - cut, o, n, 4, dx) for p, o, n, dx in runs_a[2:]]))
    return [p for p, _ in pieces], [r for _, r in pieces]


def slots_of(target_rows, slots, tokens):
    at = lax.broadcasted_iota(jnp.int32, (slots, tokens), 0)
    hit = (at == target_rows[0:1, :]) | (at == target_rows[1:2, :])
    return jnp.where(hit, 1.0, 0.0).astype(BF16)


def project_kernel(where, attn, x, gain, target_rows, *refs):
    w, (hidden, send) = refs[:-2], refs[-2:]
    y, core = where[1], where[2]
    half = attn.shape[2] // 2
    total = x[...].astype(F32)
    summed = jnp.zeros(x.shape, F32)
    for flip in (0, 1):
        own, ahead, behind, first, second = w[5 * flip : 5 * flip + 5]
        c = core if flip == 0 else 1 - core
        for part, d in ((own, 0), (ahead, 3), (behind, 1)):
            summed = summed + nn(attn[lax.rem(y + d, NY) * 2 + c], part[...])
        rows = attn[lax.rem(y + 2, NY) * 2 + c]
        summed = summed + nn(rows[:, :half], first[...]) + nn(rows[:, half:], second[...])
    state = (total + summed).astype(BF16)
    hidden[...] = state
    wide = state.astype(F32)
    rstd = lax.rsqrt(jnp.mean(wide * wide, axis=-1, keepdims=True) + norm_eps)
    moe_in = (wide * rstd * gain[...]).astype(BF16)
    place = slots_of(target_rows, send.shape[0], x.shape[0])
    send[...] = nn(place, moe_in).astype(BF16)


def project_dispatch(where, attn, x, gain, target_rows, w, slots):
    tokens, width = x.shape
    return pl.pallas_call(
        project_kernel,
        out_shape=(
            jax.ShapeDtypeStruct((tokens, width), BF16),
            jax.ShapeDtypeStruct((slots, width), BF16),
        ),
        in_specs=[SMEM] + [VMEM] * (4 + len(w)),
        out_specs=(VMEM, VMEM),
        compiler_params=params(24),
        cost_estimate=pl.CostEstimate(flops=2**30, bytes_accessed=10 * 2**20, transcendentals=0),
    )(where, attn, x, gain, target_rows, *w)


def scatter_kernel(rows, target_rows, send):
    place = slots_of(target_rows, send.shape[0], rows.shape[0])
    send[...] = nn(place, rows[...]).astype(BF16)


def scatter_rows(rows, target_rows, slots):
    return pl.pallas_call(
        scatter_kernel,
        out_shape=jax.ShapeDtypeStruct((slots, rows.shape[1]), BF16),
        in_specs=[VMEM] * 2,
        out_specs=VMEM,
        compiler_params=params(16),
        cost_estimate=pl.CostEstimate(flops=2 * slots * 64 * 2048, bytes_accessed=2**20, transcendentals=0),
    )(rows, target_rows)


def expert_kernel(part, runs, where, rows_in, rows_grad, chunk, *refs):
    extras, (both, wg, wu, wd, ga, ua, ba, hid, gpg, gpu, sems, extra_sem) = refs[: len(runs)], refs[len(runs) :]
    shards = chunk.shape[0]
    seq = where[0]
    z, x = seq // NX, lax.rem(seq, NX)
    mats = (wg, wu)
    group = 4
    steps = shards // group
    span = group * part
    some = chunk.shape[1] - part

    def start(s, _):
        row = pl.multiple_of(s * part, part)
        pltpu.make_async_copy(chunk.at[s, pl.ds(0, part)], wg.at[pl.ds(row, part)], sems.at[s // group]).start()
        pltpu.make_async_copy(chunk.at[s, pl.ds(part, some)], wu.at[pl.ds(row, some)], sems.at[steps]).start()
        return 0

    lax.fori_loop(0, shards, start, 0)
    for piece, listed in zip(extras, runs):
        for first, offset, count, dz, dx in listed:
            source = lax.rem(z + NZ - dz, NZ) * NX + lax.rem(x + NX - dx, NX)
            base = pl.multiple_of(source * part, part)
            of_up = max(0, min(part - some - offset, count))
            for mat, skip, size, at in (
                (wu, 0, of_up, some + offset),
                (wd, of_up, count - of_up, offset + of_up - (part - some)),
            ):
                if size:
                    pltpu.make_async_copy(
                        piece.at[pl.ds(first + skip, size)], mat.at[pl.ds(base + at, size)], extra_sem
                    ).start()

    for k in range(steps):
        cols = pl.ds(k * span, span)
        pltpu.make_async_copy(wg.at[cols], wg.at[cols], sems.at[k]).wait()
        term = nn(rows_in[:, cols], wg[cols, :])
        ga[...] = term if k == 0 else ga[...] + term
    view = wu.at[pl.ds(0, shards * some)]
    pltpu.make_async_copy(view, view, sems.at[steps]).wait()
    pltpu.make_async_copy(chunk, chunk, extra_sem).wait()
    for k in range(steps):
        cols = pl.ds(k * span, span)
        for rows, mat, acc in ((rows_in, wu, ua), (rows_grad, wd, ba)):
            term = nn(rows[:, cols], mat[cols, :])
            acc[...] = term if k == 0 else acc[...] + term

    def point(i, _):
        r = pl.ds(pl.multiple_of(i * 16, 16), 16)
        gate, up, grad = ga[r, :], ua[r, :], ba[r, :]
        sigma = jax.nn.sigmoid(gate)
        act = gate * sigma
        hid[r, :] = (act * up).astype(BF16)
        gpg[r, :] = (grad * up * sigma * (1.0 + gate * (1.0 - sigma))).astype(BF16)
        gpu[r, :] = (grad * act).astype(BF16)
        return 0

    lax.fori_loop(0, hid.shape[0] // 16, point, 0)
    sources = 2 * NY

    def finish(k, _):
        cols = pl.ds(pl.multiple_of(k * span, span), span)
        out = nt(hid[...], wd[cols, :]).reshape(sources, SLOT, span)
        back = (nt(gpg[...], wg[cols, :]) + nt(gpu[...], wu[cols, :])).reshape(sources, SLOT, span)
        rest = jnp.zeros((sources, BACK - 2 * CAP, span), F32)
        joined = jnp.concatenate([out[:, :CAP], back[:, :CAP], rest], axis=1)
        both[:, cols] = joined.reshape(sources * BACK, span).astype(BF16)
        return 0

    lax.fori_loop(0, steps, finish, 0)


def experts(where, rows_in, rows_grad, chunk, extras, runs):
    rows, width = rows_in.shape
    shards, depth, hidden = chunk.shape
    part = width // shards
    return pl.pallas_call(
        functools.partial(expert_kernel, part, runs),
        out_shape=jax.ShapeDtypeStruct((2 * NY * BACK, width), BF16),
        in_specs=[SMEM, VMEM, VMEM, HBM] + [VMEM] * len(extras),
        out_specs=VMEM,
        scratch_shapes=[pltpu.VMEM((width, hidden), BF16)] * 3
        + [pltpu.VMEM((rows, hidden), F32)] * 3
        + [pltpu.VMEM((rows, hidden), BF16)] * 3
        + [pltpu.SemaphoreType.DMA((shards // 4 + 1,)), pltpu.SemaphoreType.DMA(())],
        compiler_params=params(30),
        cost_estimate=pl.CostEstimate(
            flops=12 * rows * width * hidden, bytes_accessed=20 * 2**20, transcendentals=rows * hidden
        ),
    )(where, rows_in, rows_grad, chunk, *extras)


def combine_kernel(hidden, grad_out, rows, target, prob, gain, layer_out, grad_in, grad_gate):
    tokens = hidden.shape[0]
    at = lax.broadcasted_iota(jnp.int32, (tokens, rows.shape[0]), 1)

    def picked(c, offset):
        place = jnp.where(at == target[:, c : c + 1] + offset, 1.0, 0.0).astype(BF16)
        return nn(place, rows[...])

    wide = hidden[...].astype(F32)
    grad = grad_out[...].astype(F32)
    out0, out1 = picked(0, 0), picked(1, 0)
    p0, p1 = prob[:, 0:1], prob[:, 1:2]
    layer_out[...] = (wide + (p0 * out0 + p1 * out1)).astype(BF16)
    grad_gate[:, 0:1] = jnp.sum(grad * out0, axis=-1, keepdims=True)
    grad_gate[:, 1:2] = jnp.sum(grad * out1, axis=-1, keepdims=True)
    moe_grad = p0 * picked(0, CAP) + p1 * picked(1, CAP)
    rstd = lax.rsqrt(jnp.mean(wide * wide, axis=-1, keepdims=True) + norm_eps)
    normed = wide * rstd
    scaled = moe_grad * gain[...]
    mean = jnp.mean(scaled * normed, axis=-1, keepdims=True)
    grad_in[...] = (grad + rstd * (scaled - normed * mean)).astype(BF16)


def combine(hidden, grad_out, rows, target, prob, gain):
    tokens, width = hidden.shape
    made = jax.ShapeDtypeStruct((tokens, width), BF16)
    return pl.pallas_call(
        combine_kernel,
        out_shape=(made, made, jax.ShapeDtypeStruct((tokens, 2), F32)),
        in_specs=[VMEM] * 6,
        out_specs=(VMEM,) * 3,
        compiler_params=params(24),
        cost_estimate=pl.CostEstimate(flops=2**28, bytes_accessed=3 * 2**20, transcendentals=0),
    )(hidden, grad_out, rows, target, prob, gain)


def per_device(
    x_resid, queries, key_proj, val_proj, w_out, norm_gain, w_gate, w_up, w_down, routes, gate_prob, grad_out
):
    tok_dev, width = x_resid.shape
    me_seq, me_exp = lax.axis_index("seq"), lax.axis_index("exp")
    where = jnp.stack([me_seq, me_exp // 2, me_exp % 2]).astype(jnp.int32)
    some = w_up.shape[1] // 2
    chunk = lax.all_gather(jnp.concatenate([w_gate[0], w_up[0, :some]], axis=0), "seq", axis=0)
    (k_above, k_loads), (v_above, v_loads) = to_earlier(key_proj), to_earlier(val_proj)
    sent = k_loads + v_loads
    keys = [key_proj] + earlier_shards(k_above, k_loads)
    vals = [val_proj] + earlier_shards(v_above, v_loads)
    extra_rows = jnp.concatenate([w_up[0, some:], w_down[0].T], axis=0)
    extras, runs = gather_rows(extra_rows, sent, (keys, vals))
    outs = gather_out(w_out, sent)

    flat = routes.reshape(-1)
    order = jnp.arange(flat.shape[0], dtype=jnp.int32)
    same = (flat[:, None] == flat[None, :]) & (order[None, :] < order[:, None])
    rank = jnp.sum(same.astype(jnp.int32), axis=1)
    target_rows = (flat * SLOT + rank).reshape(tok_dev, 2).T
    returned = (flat * BACK + rank).reshape(tok_dev, 2)
    sources = 2 * NY
    slots = sources * SLOT
    gain = norm_gain[None, :]

    def exchange(rows):
        split = rows.reshape(sources, rows.shape[0] // sources, rows.shape[1])
        return lax.all_to_all(split, "exp", split_axis=0, concat_axis=0, tiled=True)

    recv_grad = exchange(scatter_rows(after(grad_out, sent), target_rows, slots)).reshape(slots, width)
    attn = exchange(attention(where, queries, keys, vals))
    hidden, send_in = project_dispatch(where, attn, x_resid, gain, target_rows, outs, slots)
    recv_in = exchange(send_in).reshape(slots, width)
    both = experts(where, recv_in, recv_grad, chunk, extras, runs)
    rows = exchange(both).reshape(sources * BACK, width)
    return combine(hidden, grad_out, rows, returned, gate_prob, gain)


def solution(mesh):
    tokens = P(("seq", "exp"), None)
    heads = P("seq", "exp")
    placed = (
        tokens,
        heads,
        heads,
        heads,
        P("exp", None),
        P(),
        P("exp", "seq", None),
        P("exp", "seq", None),
        P("exp", None, "seq"),
        tokens,
        tokens,
        tokens,
    )
    return jax.shard_map(
        per_device, mesh=mesh, in_specs=placed, out_specs=(tokens, tokens, tokens), check_vma=False
    )
```

```python
import functools
import math

import jax
import jax.numpy as jnp
from jax import lax
from jax.experimental import pallas as pl
from jax.experimental.pallas import tpu as pltpu
from jax.sharding import PartitionSpec as P

HD = 128
W = 2048
CAP = 18
SLOT = 24
BACK = 40
NZ = 8
NX = 4
NY = 4
norm_eps = 1e-06
F32 = jnp.float32
BF16 = jnp.bfloat16
VMEM = pl.BlockSpec(memory_space=pltpu.VMEM)
SMEM = pl.BlockSpec(memory_space=pltpu.SMEM)
HBM = pl.BlockSpec(memory_space=pltpu.HBM)


def params(mib):
    return pltpu.CompilerParams(vmem_limit_bytes=mib * 2**20)


def nt(a, b):
    return lax.dot_general(a, b, (((1,), (1,)), ((), ())), preferred_element_type=F32)


def nn(a, b):
    return jnp.dot(a, b, preferred_element_type=F32)


def shift_zx(block, dz, dx):
    route = [(s, ((s // NX + dz) % NZ) * NX + (s % NX + dx) % NX) for s in range(NZ * NX)]
    return lax.ppermute(block, "seq", route)


def along_z(block, d):
    return shift_zx(block, d, 0)


def along_x(block, d):
    return shift_zx(block, 0, d)


def along_y(block, d):
    return lax.ppermute(block, "exp", [(i, (i + 2 * d) % (2 * NY)) for i in range(2 * NY)])


def swap_core(block):
    return lax.ppermute(block, "exp", [(i, i ^ 1) for i in range(2 * NY)])


def after(value, *earlier):
    return lax.optimization_barrier((value, earlier))[0]


def opposite(ahead, behind, cut, move):
    return [move(ahead[:cut], 1), move(behind[cut:], -1)]


def to_earlier(own):
    x = lax.axis_index("seq") % NX
    above = along_z(own, 1)
    return above, (
        jnp.where(x == NX - 1, above, own),
        jnp.where(x < 2, own, above),
        jnp.where(x == 0, own, above),
    )


def earlier_shards(above, loads):
    return [along_x(loads[0], 1), along_x(loads[1], 2), along_x(loads[2], -1), above]


def attention_kernel(where, q, k0, k1, k2, k3, k4, v0, v1, v2, v3, v4, out):
    keys, vals = (k0, k1, k2, k3, k4), (v0, v1, v2, v3, v4)
    rows, span = 128, k0.shape[0]
    scale = 1.0 / math.sqrt(HD)
    seq = where[0]

    def block(i, _):
        at = pl.multiple_of(i * rows, rows)
        qpos = at + lax.broadcasted_iota(jnp.int32, (rows, span), 0)
        kpos = lax.broadcasted_iota(jnp.int32, (rows, span), 1)
        for h in range(out.shape[1] // HD):
            cols = slice(h * HD, (h + 1) * HD)
            queries = q[pl.ds(at, rows), cols]
            scores = []
            for d in range(5):
                s = nt(queries, keys[d][:, cols]) * scale
                if d == 0:
                    s = jnp.where(kpos <= qpos, s, -jnp.inf)
                elif d == 4:
                    s = jnp.where((kpos > qpos) & (seq >= d), s, -jnp.inf)
                else:
                    s = jnp.where(seq >= d, s, -jnp.inf)
                scores.append(s)
            top = scores[0]
            for s in scores[1:]:
                top = jnp.maximum(top, s)
            top = jnp.max(top, axis=-1, keepdims=True)
            mixed = jnp.zeros((rows, HD), F32)
            total = jnp.zeros((rows, span), F32)
            for d in range(5):
                e = jnp.exp(scores[d] - top)
                total = total + e
                mixed = mixed + nn(e.astype(BF16), vals[d][:, cols])
            out[pl.ds(at, rows), cols] = (mixed / jnp.sum(total, axis=-1, keepdims=True)).astype(BF16)
        return 0

    lax.fori_loop(0, q.shape[0] // rows, block, 0)


def attention(where, q, keys, vals):
    return pl.pallas_call(
        attention_kernel,
        out_shape=jax.ShapeDtypeStruct(q.shape, BF16),
        in_specs=[SMEM] + [VMEM] * 11,
        out_specs=VMEM,
        compiler_params=params(24),
        cost_estimate=pl.CostEstimate(flops=4 * 512 * 2560 * 256, bytes_accessed=6 * 2**20, transcendentals=512 * 2560 * 2),
    )(where, q, *keys, *vals)


def gather_rows(rows, sent, arrived):
    half = rows.shape[0] // 2
    early = half // 2
    a, b = rows[:half], rows[half:]
    ax, bx = along_x(a, 1), along_x(a, -1)
    up, dn = [along_z(b, 1)], [along_z(b, -1)]
    plane = jnp.concatenate([a, ax, bx] + opposite(after(ax, sent), after(bx, sent), early, along_x), axis=0)
    up.append(along_z(after(up[0], sent), 1))
    dn.append(along_z(after(dn[0], sent), -1))
    ahead, behind = [along_z(plane, 1)], [along_z(plane, -1)]
    up.append(along_z(up[1], 1))
    dn.append(along_z(dn[1], -1))
    column = jnp.concatenate(
        [b, up[0], dn[0], up[1], dn[1], up[2], dn[2]] + opposite(up[2], dn[2], early, along_z), axis=0
    )
    runs_a = [(0, 0, half, 0), (half, 0, half, 1), (2 * half, 0, half, 3), (3 * half, 0, half, 2)]
    runs_b = [(i * half, half, half, dz) for i, dz in enumerate((0, 1, 7, 2, 6, 3, 5, 4))]
    pieces = [(plane, [(p, o, n, 0, dx) for p, o, n, dx in runs_a])]
    pieces.append((column, [(p, o, n, dz, 0) for p, o, n, dz in runs_b]))
    column = after(column, arrived)
    right, left = along_x(column, 1), along_x(column, -1)
    for _ in range(2):
        ahead.append(along_z(ahead[-1], 1))
        behind.append(along_z(behind[-1], -1))
    cut = column.shape[0] // 2
    far = opposite(right, left, cut, along_x)
    pieces.append((right, [(p, o, n, dz, 1) for p, o, n, dz in runs_b]))
    pieces.append((left, [(p, o, n, dz, 3) for p, o, n, dz in runs_b]))
    pieces.append((far[0], [(p, o, n, dz, 2) for p, o, n, dz in runs_b[:4]]))
    pieces.append((far[1], [(p - cut, o, n, dz, 2) for p, o, n, dz in runs_b[4:]]))
    for i in range(3):
        pieces.append((ahead[i], [(p, o, n, 1 + i, dx) for p, o, n, dx in runs_a]))
        pieces.append((behind[i], [(p, o, n, NZ - 1 - i, dx) for p, o, n, dx in runs_a]))
    cut = plane.shape[0] // 2
    far = opposite(ahead[2], behind[2], cut, along_z)
    pieces.append((far[0], [(p, o, n, 4, dx) for p, o, n, dx in runs_a[:2]]))
    pieces.append((far[1], [(p - cut, o, n, 4, dx) for p, o, n, dx in runs_a[2:]]))
    return [p for p, _ in pieces], [r for _, r in pieces]


def project_kernel(where, own, sib, w_own, w_sib, out):
    for d in range(NY):
        y = lax.rem(where[0] + d, NY)
        out[d] = (nn(own[y], w_own[...]) + nn(sib[y], w_sib[...])).astype(BF16)


def project(where, own, sib, w_own, w_sib):
    return pl.pallas_call(
        project_kernel,
        out_shape=jax.ShapeDtypeStruct((NY, own.shape[1], w_own.shape[1]), BF16),
        in_specs=[pl.BlockSpec(memory_space=pltpu.SMEM)] + [VMEM] * 4,
        out_specs=VMEM,
        compiler_params=params(24),
        cost_estimate=pl.CostEstimate(flops=2 * 256 * 512 * 2048, bytes_accessed=6 * 2**20, transcendentals=0),
    )(where, own, sib, w_own, w_sib)


def slots_of(target_rows, slots, tokens):
    at = lax.broadcasted_iota(jnp.int32, (slots, tokens), 0)
    hit = (at == target_rows[0:1, :]) | (at == target_rows[1:2, :])
    return jnp.where(hit, 1.0, 0.0).astype(BF16)


def norm_kernel(x, p0, p1, p2, p3, gain, target_rows, hidden, send):
    total = p0[...].astype(F32) + p1[...].astype(F32) + p2[...].astype(F32) + p3[...].astype(F32)
    state = (x[...].astype(F32) + total).astype(BF16)
    hidden[...] = state
    wide = state.astype(F32)
    rstd = lax.rsqrt(jnp.mean(wide * wide, axis=-1, keepdims=True) + norm_eps)
    moe_in = (wide * rstd * gain[...]).astype(BF16)
    place = slots_of(target_rows, send.shape[0], x.shape[0])
    send[...] = nn(place, moe_in).astype(BF16)


def norm_dispatch(x, parts, gain, target_rows, slots):
    tokens, width = x.shape
    return pl.pallas_call(
        norm_kernel,
        out_shape=(
            jax.ShapeDtypeStruct((tokens, width), BF16),
            jax.ShapeDtypeStruct((slots, width), BF16),
        ),
        in_specs=[VMEM] * 7,
        out_specs=(VMEM, VMEM),
        compiler_params=params(24),
        cost_estimate=pl.CostEstimate(flops=2 * slots * tokens * width, bytes_accessed=3 * 2**20, transcendentals=0),
    )(x, *parts, gain, target_rows)


def scatter_kernel(rows, target_rows, send):
    place = slots_of(target_rows, send.shape[0], rows.shape[0])
    send[...] = nn(place, rows[...]).astype(BF16)


def scatter_rows(rows, target_rows, slots):
    return pl.pallas_call(
        scatter_kernel,
        out_shape=jax.ShapeDtypeStruct((slots, rows.shape[1]), BF16),
        in_specs=[VMEM] * 2,
        out_specs=VMEM,
        compiler_params=params(16),
        cost_estimate=pl.CostEstimate(flops=2 * slots * 64 * 2048, bytes_accessed=2**20, transcendentals=0),
    )(rows, target_rows)


def expert_kernel(part, runs, where, rows_in, rows_grad, chunk, *refs):
    downs, (both, wg, wu, wd, ga, ua, ba, hid, gpg, gpu, sems, down_sem) = refs[: len(runs)], refs[len(runs) :]
    shards = chunk.shape[0]
    seq = where[0]
    z, x = seq // NX, lax.rem(seq, NX)
    mats = (wg, wu)
    group = 4
    steps = shards // group
    span = group * part

    def start(s, _):
        for m in range(2):
            pltpu.make_async_copy(
                chunk.at[s, pl.ds(m * part, part)],
                mats[m].at[pl.ds(pl.multiple_of(s * part, part), part)],
                sems.at[m, s // group],
            ).start()
        return 0

    lax.fori_loop(0, shards, start, 0)
    for piece, listed in zip(downs, runs):
        for first, offset, count, dz, dx in listed:
            source = lax.rem(z + NZ - dz, NZ) * NX + lax.rem(x + NX - dx, NX)
            row = pl.multiple_of(source * part + offset, 16)
            pltpu.make_async_copy(piece.at[pl.ds(first, count)], wd.at[pl.ds(row, count)], down_sem).start()

    for k in range(steps):
        cols = pl.ds(k * span, span)
        for m, acc in ((0, ga), (1, ua)):
            view = mats[m].at[cols]
            pltpu.make_async_copy(view, view, sems.at[m, k]).wait()
            term = nn(rows_in[:, cols], mats[m][cols, :])
            acc[...] = term if k == 0 else acc[...] + term
    pltpu.make_async_copy(wd, wd, down_sem).wait()
    for k in range(steps):
        cols = pl.ds(k * span, span)
        term = nn(rows_grad[:, cols], wd[cols, :])
        ba[...] = term if k == 0 else ba[...] + term

    def point(i, _):
        r = pl.ds(pl.multiple_of(i * 16, 16), 16)
        gate, up, grad = ga[r, :], ua[r, :], ba[r, :]
        sigma = jax.nn.sigmoid(gate)
        act = gate * sigma
        hid[r, :] = (act * up).astype(BF16)
        gpg[r, :] = (grad * up * sigma * (1.0 + gate * (1.0 - sigma))).astype(BF16)
        gpu[r, :] = (grad * act).astype(BF16)
        return 0

    lax.fori_loop(0, hid.shape[0] // 16, point, 0)
    sources = 2 * NY

    def finish(k, _):
        cols = pl.ds(pl.multiple_of(k * span, span), span)
        out = nt(hid[...], wd[cols, :]).reshape(sources, SLOT, span)
        back = (nt(gpg[...], wg[cols, :]) + nt(gpu[...], wu[cols, :])).reshape(sources, SLOT, span)
        rest = jnp.zeros((sources, BACK - 2 * CAP, span), F32)
        joined = jnp.concatenate([out[:, :CAP], back[:, :CAP], rest], axis=1)
        both[:, cols] = joined.reshape(sources * BACK, span).astype(BF16)
        return 0

    lax.fori_loop(0, steps, finish, 0)


def experts(where, rows_in, rows_grad, chunk, downs, runs):
    rows, width = rows_in.shape
    shards, depth, hidden = chunk.shape
    part = depth // 2
    return pl.pallas_call(
        functools.partial(expert_kernel, part, runs),
        out_shape=jax.ShapeDtypeStruct((2 * NY * BACK, width), BF16),
        in_specs=[SMEM, VMEM, VMEM] + [HBM] * (1 + len(downs)),
        out_specs=VMEM,
        scratch_shapes=[pltpu.VMEM((width, hidden), BF16)] * 3
        + [pltpu.VMEM((rows, hidden), F32)] * 3
        + [pltpu.VMEM((rows, hidden), BF16)] * 3
        + [pltpu.SemaphoreType.DMA((2, shards // 4)), pltpu.SemaphoreType.DMA(())],
        compiler_params=params(40),
        cost_estimate=pl.CostEstimate(
            flops=12 * rows * width * hidden, bytes_accessed=20 * 2**20, transcendentals=rows * hidden
        ),
    )(where, rows_in, rows_grad, chunk, *downs)


def combine_kernel(hidden, grad_out, rows, target, prob, gain, layer_out, grad_in, grad_gate):
    tokens = hidden.shape[0]
    at = lax.broadcasted_iota(jnp.int32, (tokens, rows.shape[0]), 1)

    def picked(c, offset):
        place = jnp.where(at == target[:, c : c + 1] + offset, 1.0, 0.0).astype(BF16)
        return nn(place, rows[...])

    wide = hidden[...].astype(F32)
    grad = grad_out[...].astype(F32)
    out0, out1 = picked(0, 0), picked(1, 0)
    p0, p1 = prob[:, 0:1], prob[:, 1:2]
    layer_out[...] = (wide + (p0 * out0 + p1 * out1)).astype(BF16)
    grad_gate[:, 0:1] = jnp.sum(grad * out0, axis=-1, keepdims=True)
    grad_gate[:, 1:2] = jnp.sum(grad * out1, axis=-1, keepdims=True)
    moe_grad = p0 * picked(0, CAP) + p1 * picked(1, CAP)
    rstd = lax.rsqrt(jnp.mean(wide * wide, axis=-1, keepdims=True) + norm_eps)
    normed = wide * rstd
    scaled = moe_grad * gain[...]
    mean = jnp.mean(scaled * normed, axis=-1, keepdims=True)
    grad_in[...] = (grad + rstd * (scaled - normed * mean)).astype(BF16)


def combine(hidden, grad_out, rows, target, prob, gain):
    tokens, width = hidden.shape
    made = jax.ShapeDtypeStruct((tokens, width), BF16)
    return pl.pallas_call(
        combine_kernel,
        out_shape=(made, made, jax.ShapeDtypeStruct((tokens, 2), F32)),
        in_specs=[VMEM] * 6,
        out_specs=(VMEM,) * 3,
        compiler_params=params(24),
        cost_estimate=pl.CostEstimate(flops=2**28, bytes_accessed=3 * 2**20, transcendentals=0),
    )(hidden, grad_out, rows, target, prob, gain)


def per_device(
    x_resid, queries, key_proj, val_proj, w_out, norm_gain, w_gate, w_up, w_down, routes, gate_prob, grad_out
):
    tok_dev, width = x_resid.shape
    me_seq, me_exp = lax.axis_index("seq"), lax.axis_index("exp")
    where = jnp.stack([me_seq, me_exp // 2, me_exp % 2]).astype(jnp.int32)
    core, y = me_exp % 2, me_exp // 2
    chunk = lax.all_gather(jnp.concatenate([w_gate[0], w_up[0]], axis=0), "seq", axis=0)
    (k_above, k_loads), (v_above, v_loads) = to_earlier(key_proj), to_earlier(val_proj)
    keys = [key_proj] + earlier_shards(k_above, k_loads)
    vals = [val_proj] + earlier_shards(v_above, v_loads)
    downs, runs = gather_rows(w_down[0].T, keys, (keys, vals))
    w_sib = swap_core(after(w_out, keys))

    flat = routes.reshape(-1)
    order = jnp.arange(flat.shape[0], dtype=jnp.int32)
    same = (flat[:, None] == flat[None, :]) & (order[None, :] < order[:, None])
    rank = jnp.sum(same.astype(jnp.int32), axis=1)
    target_rows = (flat * SLOT + rank).reshape(tok_dev, 2).T
    returned = (flat * BACK + rank).reshape(tok_dev, 2)
    sources = 2 * NY
    slots = sources * SLOT
    gain = norm_gain[None, :]

    def exchange(rows):
        split = rows.reshape(sources, rows.shape[0] // sources, rows.shape[1])
        return lax.all_to_all(split, "exp", split_axis=0, concat_axis=0, tiled=True)

    recv_grad = exchange(scatter_rows(after(grad_out, keys), target_rows, slots)).reshape(slots, width)
    attn = attention(where, queries, keys, vals)
    owners = attn.reshape(NY, 2, tok_dev, attn.shape[1])
    mine = lax.dynamic_index_in_dim(owners, core, 1, keepdims=False)
    theirs = swap_core(lax.dynamic_index_in_dim(owners, 1 - core, 1, keepdims=False))
    partial = project(y[None].astype(jnp.int32), mine, theirs, w_out, w_sib)
    parts = [partial[0]] + [along_y(partial[d], d) for d in (1, 2, 3)]
    hidden, send_in = norm_dispatch(x_resid, parts, gain, target_rows, slots)
    recv_in = exchange(send_in).reshape(slots, width)
    both = experts(where, recv_in, recv_grad, chunk, downs, runs)
    rows = exchange(both).reshape(sources * BACK, width)
    return combine(hidden, grad_out, rows, returned, gate_prob, gain)


def solution(mesh):
    tokens = P(("seq", "exp"), None)
    heads = P("seq", "exp")
    placed = (
        tokens,
        heads,
        heads,
        heads,
        P("exp", None),
        P(),
        P("exp", "seq", None),
        P("exp", "seq", None),
        P("exp", None, "seq"),
        tokens,
        tokens,
        tokens,
    )
    return jax.shard_map(
        per_device, mesh=mesh, in_specs=placed, out_specs=(tokens, tokens, tokens), check_vma=False
    )
```

```python
import functools
import math

import jax
import jax.numpy as jnp
from jax import lax
from jax.experimental import pallas as pl
from jax.experimental.pallas import tpu as pltpu
from jax.sharding import PartitionSpec as P

HD = 128
W = 2048
CAP = 18
SLOT = 24
BACK = 40
NZ = 8
NX = 4
NY = 4
norm_eps = 1e-06
F32 = jnp.float32
BF16 = jnp.bfloat16
VMEM = pl.BlockSpec(memory_space=pltpu.VMEM)
SMEM = pl.BlockSpec(memory_space=pltpu.SMEM)
HBM = pl.BlockSpec(memory_space=pltpu.HBM)


def params(mib):
    return pltpu.CompilerParams(vmem_limit_bytes=mib * 2**20)


def nt(a, b):
    return lax.dot_general(a, b, (((1,), (1,)), ((), ())), preferred_element_type=F32)


def nn(a, b):
    return jnp.dot(a, b, preferred_element_type=F32)


def shift_zx(block, dz, dx):
    route = [(s, ((s // NX + dz) % NZ) * NX + (s % NX + dx) % NX) for s in range(NZ * NX)]
    return lax.ppermute(block, "seq", route)


def along_z(block, d):
    return shift_zx(block, d, 0)


def along_x(block, d):
    return shift_zx(block, 0, d)


def along_y(block, d):
    return lax.ppermute(block, "exp", [(i, (i + 2 * d) % (2 * NY)) for i in range(2 * NY)])


def swap_core(block):
    return lax.ppermute(block, "exp", [(i, i ^ 1) for i in range(2 * NY)])


def after(value, *earlier):
    return lax.optimization_barrier((value, earlier))[0]


def opposite(ahead, behind, cut, move):
    return [move(ahead[:cut], 1), move(behind[cut:], -1)]


def to_earlier(own):
    x = lax.axis_index("seq") % NX
    above = along_z(own, 1)
    return above, (
        jnp.where(x == NX - 1, above, own),
        jnp.where(x < 2, own, above),
        jnp.where(x == 0, own, above),
    )


def earlier_shards(above, loads):
    return [along_x(loads[0], 1), along_x(loads[1], 2), along_x(loads[2], -1), above]


def attention_kernel(where, q, k0, k1, k2, k3, k4, v0, v1, v2, v3, v4, out):
    keys, vals = (k0, k1, k2, k3, k4), (v0, v1, v2, v3, v4)
    rows, span = 128, k0.shape[0]
    scale = 1.0 / math.sqrt(HD)
    seq = where[0]

    def block(i, _):
        at = pl.multiple_of(i * rows, rows)
        qpos = at + lax.broadcasted_iota(jnp.int32, (rows, span), 0)
        kpos = lax.broadcasted_iota(jnp.int32, (rows, span), 1)
        for h in range(out.shape[1] // HD):
            cols = slice(h * HD, (h + 1) * HD)
            queries = q[pl.ds(at, rows), cols]
            scores = []
            for d in range(5):
                s = nt(queries, keys[d][:, cols]) * scale
                if d == 0:
                    s = jnp.where(kpos <= qpos, s, -jnp.inf)
                elif d == 4:
                    s = jnp.where((kpos > qpos) & (seq >= d), s, -jnp.inf)
                else:
                    s = jnp.where(seq >= d, s, -jnp.inf)
                scores.append(s)
            top = scores[0]
            for s in scores[1:]:
                top = jnp.maximum(top, s)
            top = jnp.max(top, axis=-1, keepdims=True)
            mixed = jnp.zeros((rows, HD), F32)
            total = jnp.zeros((rows, span), F32)
            for d in range(5):
                e = jnp.exp(scores[d] - top)
                total = total + e
                mixed = mixed + nn(e.astype(BF16), vals[d][:, cols])
            out[pl.ds(at, rows), cols] = (mixed / jnp.sum(total, axis=-1, keepdims=True)).astype(BF16)
        return 0

    lax.fori_loop(0, q.shape[0] // rows, block, 0)


def attention(where, q, keys, vals):
    return pl.pallas_call(
        attention_kernel,
        out_shape=jax.ShapeDtypeStruct(q.shape, BF16),
        in_specs=[SMEM] + [VMEM] * 11,
        out_specs=VMEM,
        compiler_params=params(24),
        cost_estimate=pl.CostEstimate(flops=4 * 512 * 2560 * 256, bytes_accessed=6 * 2**20, transcendentals=512 * 2560 * 2),
    )(where, q, *keys, *vals)


def gather_rows(rows, earlier):
    count = rows.shape[0]
    plane = jnp.concatenate([rows, along_x(rows, 1), along_x(rows, 2), along_x(rows, -1)], axis=0)
    plane = after(plane, earlier)
    pieces = [(plane, 0)]
    ahead, behind = plane, plane
    for dz in (1, 2, 3):
        ahead, behind = along_z(ahead, 1), along_z(behind, -1)
        pieces += [(ahead, dz), (behind, NZ - dz)]
    listed = [[(dx * count, dz, dx) for dx in range(NX)] for _, dz in pieces]
    far = opposite(ahead, behind, NX // 2 * count, along_z)
    listed += [[(dx % 2 * count, NZ // 2, dx) for dx in pair] for pair in ((0, 1), (2, 3))]
    return [p for p, _ in pieces] + far, listed


def project_kernel(where, own, sib, w_own, w_sib, out):
    for d in range(NY):
        y = lax.rem(where[0] + d, NY)
        out[d] = (nn(own[y], w_own[...]) + nn(sib[y], w_sib[...])).astype(BF16)


def project(where, own, sib, w_own, w_sib):
    return pl.pallas_call(
        project_kernel,
        out_shape=jax.ShapeDtypeStruct((NY, own.shape[1], w_own.shape[1]), BF16),
        in_specs=[pl.BlockSpec(memory_space=pltpu.SMEM)] + [VMEM] * 4,
        out_specs=VMEM,
        compiler_params=params(24),
        cost_estimate=pl.CostEstimate(flops=2 * 256 * 512 * 2048, bytes_accessed=6 * 2**20, transcendentals=0),
    )(where, own, sib, w_own, w_sib)


def slots_of(target_rows, slots, tokens):
    at = lax.broadcasted_iota(jnp.int32, (slots, tokens), 0)
    hit = (at == target_rows[0:1, :]) | (at == target_rows[1:2, :])
    return jnp.where(hit, 1.0, 0.0).astype(BF16)


def norm_kernel(x, p0, p1, p2, p3, gain, target_rows, hidden, send):
    total = p0[...].astype(F32) + p1[...].astype(F32) + p2[...].astype(F32) + p3[...].astype(F32)
    state = (x[...].astype(F32) + total).astype(BF16)
    hidden[...] = state
    wide = state.astype(F32)
    rstd = lax.rsqrt(jnp.mean(wide * wide, axis=-1, keepdims=True) + norm_eps)
    moe_in = (wide * rstd * gain[...]).astype(BF16)
    place = slots_of(target_rows, send.shape[0], x.shape[0])
    send[...] = nn(place, moe_in).astype(BF16)


def norm_dispatch(x, parts, gain, target_rows, slots):
    tokens, width = x.shape
    return pl.pallas_call(
        norm_kernel,
        out_shape=(
            jax.ShapeDtypeStruct((tokens, width), BF16),
            jax.ShapeDtypeStruct((slots, width), BF16),
        ),
        in_specs=[VMEM] * 7,
        out_specs=(VMEM, VMEM),
        compiler_params=params(24),
        cost_estimate=pl.CostEstimate(flops=2 * slots * tokens * width, bytes_accessed=3 * 2**20, transcendentals=0),
    )(x, *parts, gain, target_rows)


def scatter_kernel(rows, target_rows, send):
    place = slots_of(target_rows, send.shape[0], rows.shape[0])
    send[...] = nn(place, rows[...]).astype(BF16)


def scatter_rows(rows, target_rows, slots):
    return pl.pallas_call(
        scatter_kernel,
        out_shape=jax.ShapeDtypeStruct((slots, rows.shape[1]), BF16),
        in_specs=[VMEM] * 2,
        out_specs=VMEM,
        compiler_params=params(16),
        cost_estimate=pl.CostEstimate(flops=2 * slots * 64 * 2048, bytes_accessed=2**20, transcendentals=0),
    )(rows, target_rows)


def down_kernel(runs, where, rows_grad, *refs):
    pieces, (wd, back, sem) = refs[: len(runs)], refs[len(runs) :]
    seq = where[0]
    z, x = seq // NX, lax.rem(seq, NX)
    part = wd.shape[0] // (NZ * NX)
    for piece, listed in zip(pieces, runs):
        for first, dz, dx in listed:
            source = lax.rem(z + NZ - dz, NZ) * NX + lax.rem(x + NX - dx, NX)
            row = pl.multiple_of(source * part, part)
            pltpu.make_async_copy(piece.at[pl.ds(first, part)], wd.at[pl.ds(row, part)], sem).start()
    pltpu.make_async_copy(wd, wd, sem).wait()
    span = 256
    for k in range(wd.shape[0] // span):
        cols = pl.ds(k * span, span)
        term = nn(rows_grad[:, cols], wd[cols, :])
        back[...] = term if k == 0 else back[...] + term


def down_part(where, rows_grad, pieces, runs):
    rows, width = rows_grad.shape
    hidden = pieces[0].shape[1]
    return pl.pallas_call(
        functools.partial(down_kernel, runs),
        out_shape=(jax.ShapeDtypeStruct((width, hidden), BF16), jax.ShapeDtypeStruct((rows, hidden), F32)),
        in_specs=[SMEM, VMEM] + [HBM] * len(pieces),
        out_specs=(VMEM, VMEM),
        scratch_shapes=[pltpu.SemaphoreType.DMA(())],
        compiler_params=params(16),
        cost_estimate=pl.CostEstimate(flops=2 * rows * width * hidden, bytes_accessed=7 * 2**20, transcendentals=0),
    )(where, rows_grad, *pieces)


def expert_kernel(rows_in, down, ba, chunk, both, wg, wu, wd, ga, ua, hid, gpg, gpu, sems, down_sem):
    shards = chunk.shape[0]
    part = chunk.shape[1] // 2
    mats = (wg, wu)
    group = 4
    steps = shards // group
    span = group * part

    def start(s, _):
        row = pl.multiple_of(s * part, part)
        for m in range(2):
            pltpu.make_async_copy(
                chunk.at[s, pl.ds(m * part, part)], mats[m].at[pl.ds(row, part)], sems.at[m, s // group]
            ).start()
        return 0

    lax.fori_loop(0, shards, start, 0)
    fetch = pltpu.make_async_copy(down, wd, down_sem)
    fetch.start()
    for k in range(steps):
        cols = pl.ds(k * span, span)
        for m, acc in ((0, ga), (1, ua)):
            view = mats[m].at[cols]
            pltpu.make_async_copy(view, view, sems.at[m, k]).wait()
            term = nn(rows_in[:, cols], mats[m][cols, :])
            acc[...] = term if k == 0 else acc[...] + term

    def point(i, _):
        r = pl.ds(pl.multiple_of(i * 16, 16), 16)
        gate, up, grad = ga[r, :], ua[r, :], ba[r, :]
        sigma = jax.nn.sigmoid(gate)
        act = gate * sigma
        hid[r, :] = (act * up).astype(BF16)
        gpg[r, :] = (grad * up * sigma * (1.0 + gate * (1.0 - sigma))).astype(BF16)
        gpu[r, :] = (grad * act).astype(BF16)
        return 0

    lax.fori_loop(0, hid.shape[0] // 16, point, 0)
    fetch.wait()
    sources = 2 * NY

    def finish(k, _):
        cols = pl.ds(pl.multiple_of(k * span, span), span)
        out = nt(hid[...], wd[cols, :]).reshape(sources, SLOT, span)
        back = (nt(gpg[...], wg[cols, :]) + nt(gpu[...], wu[cols, :])).reshape(sources, SLOT, span)
        rest = jnp.zeros((sources, BACK - 2 * CAP, span), F32)
        joined = jnp.concatenate([out[:, :CAP], back[:, :CAP], rest], axis=1)
        both[:, cols] = joined.reshape(sources * BACK, span).astype(BF16)
        return 0

    lax.fori_loop(0, steps, finish, 0)


def experts(rows_in, wd, back, chunk):
    rows, width = rows_in.shape
    shards, hidden = chunk.shape[0], chunk.shape[2]
    return pl.pallas_call(
        expert_kernel,
        out_shape=jax.ShapeDtypeStruct((2 * NY * BACK, width), BF16),
        in_specs=[VMEM, HBM, VMEM, HBM],
        out_specs=VMEM,
        scratch_shapes=[pltpu.VMEM((width, hidden), BF16)] * 3
        + [pltpu.VMEM((rows, hidden), F32)] * 2
        + [pltpu.VMEM((rows, hidden), BF16)] * 3
        + [pltpu.SemaphoreType.DMA((2, shards // 4)), pltpu.SemaphoreType.DMA(())],
        compiler_params=params(50),
        cost_estimate=pl.CostEstimate(
            flops=10 * rows * width * hidden, bytes_accessed=14 * 2**20, transcendentals=rows * hidden
        ),
    )(rows_in, wd, back, chunk)


def combine_kernel(hidden, grad_out, rows, target, prob, gain, layer_out, grad_in, grad_gate):
    tokens = hidden.shape[0]
    at = lax.broadcasted_iota(jnp.int32, (tokens, rows.shape[0]), 1)

    def picked(c, offset):
        place = jnp.where(at == target[:, c : c + 1] + offset, 1.0, 0.0).astype(BF16)
        return nn(place, rows[...])

    wide = hidden[...].astype(F32)
    grad = grad_out[...].astype(F32)
    out0, out1 = picked(0, 0), picked(1, 0)
    p0, p1 = prob[:, 0:1], prob[:, 1:2]
    layer_out[...] = (wide + (p0 * out0 + p1 * out1)).astype(BF16)
    grad_gate[:, 0:1] = jnp.sum(grad * out0, axis=-1, keepdims=True)
    grad_gate[:, 1:2] = jnp.sum(grad * out1, axis=-1, keepdims=True)
    moe_grad = p0 * picked(0, CAP) + p1 * picked(1, CAP)
    rstd = lax.rsqrt(jnp.mean(wide * wide, axis=-1, keepdims=True) + norm_eps)
    normed = wide * rstd
    scaled = moe_grad * gain[...]
    mean = jnp.mean(scaled * normed, axis=-1, keepdims=True)
    grad_in[...] = (grad + rstd * (scaled - normed * mean)).astype(BF16)


def combine(hidden, grad_out, rows, target, prob, gain):
    tokens, width = hidden.shape
    made = jax.ShapeDtypeStruct((tokens, width), BF16)
    return pl.pallas_call(
        combine_kernel,
        out_shape=(made, made, jax.ShapeDtypeStruct((tokens, 2), F32)),
        in_specs=[VMEM] * 6,
        out_specs=(VMEM,) * 3,
        compiler_params=params(24),
        cost_estimate=pl.CostEstimate(flops=2**28, bytes_accessed=3 * 2**20, transcendentals=0),
    )(hidden, grad_out, rows, target, prob, gain)


def per_device(
    x_resid, queries, key_proj, val_proj, w_out, norm_gain, w_gate, w_up, w_down, routes, gate_prob, grad_out
):
    tok_dev, width = x_resid.shape
    me_seq, me_exp = lax.axis_index("seq"), lax.axis_index("exp")
    where = jnp.stack([me_seq, me_exp // 2, me_exp % 2]).astype(jnp.int32)
    core, y = me_exp % 2, me_exp // 2
    chunk = lax.all_gather(jnp.concatenate([w_gate[0], w_up[0]], axis=0), "seq", axis=0)
    (k_above, k_loads), (v_above, v_loads) = to_earlier(key_proj), to_earlier(val_proj)
    keys = [key_proj] + earlier_shards(k_above, k_loads)
    vals = [val_proj] + earlier_shards(v_above, v_loads)
    downs, runs = gather_rows(w_down[0].T, (k_above, v_above))
    w_sib = swap_core(after(w_out, keys))

    flat = routes.reshape(-1)
    order = jnp.arange(flat.shape[0], dtype=jnp.int32)
    same = (flat[:, None] == flat[None, :]) & (order[None, :] < order[:, None])
    rank = jnp.sum(same.astype(jnp.int32), axis=1)
    target_rows = (flat * SLOT + rank).reshape(tok_dev, 2).T
    returned = (flat * BACK + rank).reshape(tok_dev, 2)
    sources = 2 * NY
    slots = sources * SLOT
    gain = norm_gain[None, :]

    def exchange(rows):
        split = rows.reshape(sources, rows.shape[0] // sources, rows.shape[1])
        return lax.all_to_all(split, "exp", split_axis=0, concat_axis=0, tiled=True)

    recv_grad = exchange(scatter_rows(after(grad_out, keys), target_rows, slots)).reshape(slots, width)
    attn = attention(where, queries, keys, vals)
    owners = attn.reshape(NY, 2, tok_dev, attn.shape[1])
    mine = lax.dynamic_index_in_dim(owners, core, 1, keepdims=False)
    theirs = swap_core(lax.dynamic_index_in_dim(owners, 1 - core, 1, keepdims=False))
    partial = project(y[None].astype(jnp.int32), mine, theirs, w_out, w_sib)
    parts = [partial[0]] + [along_y(partial[d], d) for d in (1, 2, 3)]
    hidden, send_in = norm_dispatch(x_resid, parts, gain, target_rows, slots)
    recv_in = exchange(send_in).reshape(slots, width)
    both = experts(recv_in, *down_part(where, recv_grad, downs, runs), chunk)
    rows = exchange(both).reshape(sources * BACK, width)
    return combine(hidden, grad_out, rows, returned, gate_prob, gain)


def solution(mesh):
    tokens = P(("seq", "exp"), None)
    heads = P("seq", "exp")
    placed = (
        tokens,
        heads,
        heads,
        heads,
        P("exp", None),
        P(),
        P("exp", "seq", None),
        P("exp", "seq", None),
        P("exp", None, "seq"),
        tokens,
        tokens,
        tokens,
    )
    return jax.shard_map(
        per_device, mesh=mesh, in_specs=placed, out_specs=(tokens, tokens, tokens), check_vma=False
    )
```

```python
import functools
import math

import jax
import jax.numpy as jnp
from jax import lax
from jax.experimental import pallas as pl
from jax.experimental.pallas import tpu as pltpu
from jax.sharding import PartitionSpec as P

HD = 128
W = 2048
CAP = 18
SLOT = 24
BACK = 40
NZ = 8
NX = 4
NY = 4
norm_eps = 1e-06
F32 = jnp.float32
BF16 = jnp.bfloat16
VMEM = pl.BlockSpec(memory_space=pltpu.VMEM)
SMEM = pl.BlockSpec(memory_space=pltpu.SMEM)
HBM = pl.BlockSpec(memory_space=pltpu.HBM)


def params(mib):
    return pltpu.CompilerParams(vmem_limit_bytes=mib * 2**20)


def nt(a, b):
    return lax.dot_general(a, b, (((1,), (1,)), ((), ())), preferred_element_type=F32)


def nn(a, b):
    return jnp.dot(a, b, preferred_element_type=F32)


def shift_zx(block, dz, dx):
    route = [(s, ((s // NX + dz) % NZ) * NX + (s % NX + dx) % NX) for s in range(NZ * NX)]
    return lax.ppermute(block, "seq", route)


def along_z(block, d):
    return shift_zx(block, d, 0)


def along_x(block, d):
    return shift_zx(block, 0, d)


def along_y(block, d):
    return lax.ppermute(block, "exp", [(i, (i + 2 * d) % (2 * NY)) for i in range(2 * NY)])


def swap_core(block):
    return lax.ppermute(block, "exp", [(i, i ^ 1) for i in range(2 * NY)])


def after(value, *earlier):
    return lax.optimization_barrier((value, earlier))[0]


def opposite(ahead, behind, cut, move):
    return [move(ahead[:cut], 1), move(behind[cut:], -1)]


def to_earlier(own):
    x = lax.axis_index("seq") % NX
    above = along_z(own, 1)
    return above, (
        jnp.where(x == NX - 1, above, own),
        jnp.where(x < 2, own, above),
        jnp.where(x == 0, own, above),
    )


def earlier_shards(above, loads):
    return [along_x(loads[0], 1), along_x(loads[1], 2), along_x(loads[2], -1), above]


def attention_kernel(where, q, k0, k1, k2, k3, k4, v0, v1, v2, v3, v4, out):
    keys, vals = (k0, k1, k2, k3, k4), (v0, v1, v2, v3, v4)
    rows, span = 128, k0.shape[0]
    scale = 1.0 / math.sqrt(HD)
    seq = where[0]

    def block(i, _):
        at = pl.multiple_of(i * rows, rows)
        qpos = at + lax.broadcasted_iota(jnp.int32, (rows, span), 0)
        kpos = lax.broadcasted_iota(jnp.int32, (rows, span), 1)
        for h in range(out.shape[1] // HD):
            cols = slice(h * HD, (h + 1) * HD)
            queries = q[pl.ds(at, rows), cols]
            scores = []
            for d in range(5):
                s = nt(queries, keys[d][:, cols]) * scale
                if d == 0:
                    s = jnp.where(kpos <= qpos, s, -jnp.inf)
                elif d == 4:
                    s = jnp.where((kpos > qpos) & (seq >= d), s, -jnp.inf)
                else:
                    s = jnp.where(seq >= d, s, -jnp.inf)
                scores.append(s)
            top = scores[0]
            for s in scores[1:]:
                top = jnp.maximum(top, s)
            top = jnp.max(top, axis=-1, keepdims=True)
            mixed = jnp.zeros((rows, HD), F32)
            total = jnp.zeros((rows, span), F32)
            for d in range(5):
                e = jnp.exp(scores[d] - top)
                total = total + e
                mixed = mixed + nn(e.astype(BF16), vals[d][:, cols])
            out[pl.ds(at, rows), cols] = (mixed / jnp.sum(total, axis=-1, keepdims=True)).astype(BF16)
        return 0

    lax.fori_loop(0, q.shape[0] // rows, block, 0)


def attention(where, q, keys, vals):
    return pl.pallas_call(
        attention_kernel,
        out_shape=jax.ShapeDtypeStruct(q.shape, BF16),
        in_specs=[SMEM] + [VMEM] * 11,
        out_specs=VMEM,
        compiler_params=params(24),
        cost_estimate=pl.CostEstimate(flops=4 * 512 * 2560 * 256, bytes_accessed=6 * 2**20, transcendentals=512 * 2560 * 2),
    )(where, q, *keys, *vals)


def round_z(block, cut, first=None):
    ahead, behind = [along_z(block, 1)], [along_z(block, -1)]
    for i in range(2):
        a, b = ahead[-1], behind[-1]
        if i == 0 and first is not None:
            a, b = after(a, first), after(b, first)
        ahead.append(along_z(a, 1))
        behind.append(along_z(b, -1))
    return ahead, behind, opposite(ahead[2], behind[2], cut, along_z)


def gather_rows(rows, above, arrived):
    half = rows.shape[0] // 2
    a, b = rows[:half], rows[half:]
    plane = jnp.concatenate([a, along_x(a, 1), along_x(a, 2), along_x(a, -1)], axis=0)
    up, down, far = round_z(b, half // 2, above)
    column = jnp.concatenate([b] + up + down + far, axis=0)
    depths = (0, 1, 2, 3, 7, 6, 5, 4)
    plane = after(plane, up[2], down[2])
    ahead, behind, far = round_z(plane, NX // 2 * half)
    pieces = [(plane, 0)]
    for i in range(3):
        pieces += [(ahead[i], i + 1), (behind[i], NZ - 1 - i)]
    listed = [[(dx * half, 0, half, dz, dx) for dx in range(NX)] for _, dz in pieces]
    listed += [[(dx % 2 * half, 0, half, NZ // 2, dx) for dx in pair] for pair in ((0, 1), (2, 3))]
    pieces = [p for p, _ in pieces] + far
    sent = after(column, arrived)
    pieces += [column] + [along_x(sent, d) for d in (1, 2, -1)]
    listed += [[(i * half, half, half, dz, dx) for i, dz in enumerate(depths)] for dx in range(NX)]
    return pieces, listed


def project_kernel(where, own, sib, w_own, w_sib, out):
    for d in range(NY):
        y = lax.rem(where[0] + d, NY)
        out[d] = (nn(own[y], w_own[...]) + nn(sib[y], w_sib[...])).astype(BF16)


def project(where, own, sib, w_own, w_sib):
    return pl.pallas_call(
        project_kernel,
        out_shape=jax.ShapeDtypeStruct((NY, own.shape[1], w_own.shape[1]), BF16),
        in_specs=[pl.BlockSpec(memory_space=pltpu.SMEM)] + [VMEM] * 4,
        out_specs=VMEM,
        compiler_params=params(24),
        cost_estimate=pl.CostEstimate(flops=2 * 256 * 512 * 2048, bytes_accessed=6 * 2**20, transcendentals=0),
    )(where, own, sib, w_own, w_sib)


def slots_of(target_rows, slots, tokens):
    at = lax.broadcasted_iota(jnp.int32, (slots, tokens), 0)
    hit = (at == target_rows[0:1, :]) | (at == target_rows[1:2, :])
    return jnp.where(hit, 1.0, 0.0).astype(BF16)


def norm_kernel(x, p0, p1, p2, p3, gain, target_rows, hidden, send):
    total = p0[...].astype(F32) + p1[...].astype(F32) + p2[...].astype(F32) + p3[...].astype(F32)
    state = (x[...].astype(F32) + total).astype(BF16)
    hidden[...] = state
    wide = state.astype(F32)
    rstd = lax.rsqrt(jnp.mean(wide * wide, axis=-1, keepdims=True) + norm_eps)
    moe_in = (wide * rstd * gain[...]).astype(BF16)
    place = slots_of(target_rows, send.shape[0], x.shape[0])
    send[...] = nn(place, moe_in).astype(BF16)


def norm_dispatch(x, parts, gain, target_rows, slots):
    tokens, width = x.shape
    return pl.pallas_call(
        norm_kernel,
        out_shape=(
            jax.ShapeDtypeStruct((tokens, width), BF16),
            jax.ShapeDtypeStruct((slots, width), BF16),
        ),
        in_specs=[VMEM] * 7,
        out_specs=(VMEM, VMEM),
        compiler_params=params(24),
        cost_estimate=pl.CostEstimate(flops=2 * slots * tokens * width, bytes_accessed=3 * 2**20, transcendentals=0),
    )(x, *parts, gain, target_rows)


def scatter_kernel(rows, target_rows, send):
    place = slots_of(target_rows, send.shape[0], rows.shape[0])
    send[...] = nn(place, rows[...]).astype(BF16)


def scatter_rows(rows, target_rows, slots):
    return pl.pallas_call(
        scatter_kernel,
        out_shape=jax.ShapeDtypeStruct((slots, rows.shape[1]), BF16),
        in_specs=[VMEM] * 2,
        out_specs=VMEM,
        compiler_params=params(16),
        cost_estimate=pl.CostEstimate(flops=2 * slots * 64 * 2048, bytes_accessed=2**20, transcendentals=0),
    )(rows, target_rows)


def down_kernel(runs, where, rows_grad, *refs):
    pieces, (wd, back, sem) = refs[: len(runs)], refs[len(runs) :]
    seq = where[0]
    z, x = seq // NX, lax.rem(seq, NX)
    part = wd.shape[0] // (NZ * NX)
    for piece, listed in zip(pieces, runs):
        for first, offset, count, dz, dx in listed:
            source = lax.rem(z + NZ - dz, NZ) * NX + lax.rem(x + NX - dx, NX)
            row = pl.multiple_of(source * part + offset, count)
            pltpu.make_async_copy(piece.at[pl.ds(first, count)], wd.at[pl.ds(row, count)], sem).start()
    pltpu.make_async_copy(wd, wd, sem).wait()
    span = 256
    for k in range(wd.shape[0] // span):
        cols = pl.ds(k * span, span)
        term = nn(rows_grad[:, cols], wd[cols, :])
        back[...] = term if k == 0 else back[...] + term


def down_part(where, rows_grad, pieces, runs):
    rows, width = rows_grad.shape
    hidden = pieces[0].shape[1]
    return pl.pallas_call(
        functools.partial(down_kernel, runs),
        out_shape=(jax.ShapeDtypeStruct((width, hidden), BF16), jax.ShapeDtypeStruct((rows, hidden), F32)),
        in_specs=[SMEM, VMEM] + [HBM] * len(pieces),
        out_specs=(VMEM, VMEM),
        scratch_shapes=[pltpu.SemaphoreType.DMA(())],
        compiler_params=params(16),
        cost_estimate=pl.CostEstimate(flops=2 * rows * width * hidden, bytes_accessed=7 * 2**20, transcendentals=0),
    )(where, rows_grad, *pieces)


def expert_kernel(rows_in, down, ba, chunk, both, wg, wu, wd, ga, ua, hid, gpg, gpu, sems, down_sem):
    shards = chunk.shape[0]
    part = chunk.shape[1] // 2
    mats = (wg, wu)
    group = 4
    steps = shards // group
    span = group * part

    def start(s, _):
        row = pl.multiple_of(s * part, part)
        for m in range(2):
            pltpu.make_async_copy(
                chunk.at[s, pl.ds(m * part, part)], mats[m].at[pl.ds(row, part)], sems.at[m, s // group]
            ).start()
        return 0

    lax.fori_loop(0, shards, start, 0)
    fetch = pltpu.make_async_copy(down, wd, down_sem)
    fetch.start()
    for k in range(steps):
        cols = pl.ds(k * span, span)
        for m, acc in ((0, ga), (1, ua)):
            view = mats[m].at[cols]
            pltpu.make_async_copy(view, view, sems.at[m, k]).wait()
            term = nn(rows_in[:, cols], mats[m][cols, :])
            acc[...] = term if k == 0 else acc[...] + term

    def point(i, _):
        r = pl.ds(pl.multiple_of(i * 16, 16), 16)
        gate, up, grad = ga[r, :], ua[r, :], ba[r, :]
        sigma = jax.nn.sigmoid(gate)
        act = gate * sigma
        hid[r, :] = (act * up).astype(BF16)
        gpg[r, :] = (grad * up * sigma * (1.0 + gate * (1.0 - sigma))).astype(BF16)
        gpu[r, :] = (grad * act).astype(BF16)
        return 0

    lax.fori_loop(0, hid.shape[0] // 16, point, 0)
    fetch.wait()
    sources = 2 * NY

    def finish(k, _):
        cols = pl.ds(pl.multiple_of(k * span, span), span)
        out = nt(hid[...], wd[cols, :]).reshape(sources, SLOT, span)
        back = (nt(gpg[...], wg[cols, :]) + nt(gpu[...], wu[cols, :])).reshape(sources, SLOT, span)
        rest = jnp.zeros((sources, BACK - 2 * CAP, span), F32)
        joined = jnp.concatenate([out[:, :CAP], back[:, :CAP], rest], axis=1)
        both[:, cols] = joined.reshape(sources * BACK, span).astype(BF16)
        return 0

    lax.fori_loop(0, steps, finish, 0)


def experts(rows_in, wd, back, chunk):
    rows, width = rows_in.shape
    shards, hidden = chunk.shape[0], chunk.shape[2]
    return pl.pallas_call(
        expert_kernel,
        out_shape=jax.ShapeDtypeStruct((2 * NY * BACK, width), BF16),
        in_specs=[VMEM, HBM, VMEM, HBM],
        out_specs=VMEM,
        scratch_shapes=[pltpu.VMEM((width, hidden), BF16)] * 3
        + [pltpu.VMEM((rows, hidden), F32)] * 2
        + [pltpu.VMEM((rows, hidden), BF16)] * 3
        + [pltpu.SemaphoreType.DMA((2, shards // 4)), pltpu.SemaphoreType.DMA(())],
        compiler_params=params(50),
        cost_estimate=pl.CostEstimate(
            flops=10 * rows * width * hidden, bytes_accessed=14 * 2**20, transcendentals=rows * hidden
        ),
    )(rows_in, wd, back, chunk)


def combine_kernel(hidden, grad_out, rows, target, prob, gain, layer_out, grad_in, grad_gate):
    tokens = hidden.shape[0]
    at = lax.broadcasted_iota(jnp.int32, (tokens, rows.shape[0]), 1)

    def picked(c, offset):
        place = jnp.where(at == target[:, c : c + 1] + offset, 1.0, 0.0).astype(BF16)
        return nn(place, rows[...])

    wide = hidden[...].astype(F32)
    grad = grad_out[...].astype(F32)
    out0, out1 = picked(0, 0), picked(1, 0)
    p0, p1 = prob[:, 0:1], prob[:, 1:2]
    layer_out[...] = (wide + (p0 * out0 + p1 * out1)).astype(BF16)
    grad_gate[:, 0:1] = jnp.sum(grad * out0, axis=-1, keepdims=True)
    grad_gate[:, 1:2] = jnp.sum(grad * out1, axis=-1, keepdims=True)
    moe_grad = p0 * picked(0, CAP) + p1 * picked(1, CAP)
    rstd = lax.rsqrt(jnp.mean(wide * wide, axis=-1, keepdims=True) + norm_eps)
    normed = wide * rstd
    scaled = moe_grad * gain[...]
    mean = jnp.mean(scaled * normed, axis=-1, keepdims=True)
    grad_in[...] = (grad + rstd * (scaled - normed * mean)).astype(BF16)


def combine(hidden, grad_out, rows, target, prob, gain):
    tokens, width = hidden.shape
    made = jax.ShapeDtypeStruct((tokens, width), BF16)
    return pl.pallas_call(
        combine_kernel,
        out_shape=(made, made, jax.ShapeDtypeStruct((tokens, 2), F32)),
        in_specs=[VMEM] * 6,
        out_specs=(VMEM,) * 3,
        compiler_params=params(24),
        cost_estimate=pl.CostEstimate(flops=2**28, bytes_accessed=3 * 2**20, transcendentals=0),
    )(hidden, grad_out, rows, target, prob, gain)


def per_device(
    x_resid, queries, key_proj, val_proj, w_out, norm_gain, w_gate, w_up, w_down, routes, gate_prob, grad_out
):
    tok_dev, width = x_resid.shape
    me_seq, me_exp = lax.axis_index("seq"), lax.axis_index("exp")
    where = jnp.stack([me_seq, me_exp // 2, me_exp % 2]).astype(jnp.int32)
    core, y = me_exp % 2, me_exp // 2
    chunk = lax.all_gather(jnp.concatenate([w_gate[0], w_up[0]], axis=0), "seq", axis=0)
    (k_above, k_loads), (v_above, v_loads) = to_earlier(key_proj), to_earlier(val_proj)
    keys = [key_proj] + earlier_shards(k_above, k_loads)
    vals = [val_proj] + earlier_shards(v_above, v_loads)
    downs, runs = gather_rows(w_down[0].T, k_above, (keys, vals))
    w_sib = swap_core(after(w_out, keys))

    flat = routes.reshape(-1)
    order = jnp.arange(flat.shape[0], dtype=jnp.int32)
    same = (flat[:, None] == flat[None, :]) & (order[None, :] < order[:, None])
    rank = jnp.sum(same.astype(jnp.int32), axis=1)
    target_rows = (flat * SLOT + rank).reshape(tok_dev, 2).T
    returned = (flat * BACK + rank).reshape(tok_dev, 2)
    sources = 2 * NY
    slots = sources * SLOT
    gain = norm_gain[None, :]

    def exchange(rows):
        split = rows.reshape(sources, rows.shape[0] // sources, rows.shape[1])
        return lax.all_to_all(split, "exp", split_axis=0, concat_axis=0, tiled=True)

    recv_grad = exchange(scatter_rows(after(grad_out, keys), target_rows, slots)).reshape(slots, width)
    attn = attention(where, queries, keys, vals)
    owners = attn.reshape(NY, 2, tok_dev, attn.shape[1])
    mine = lax.dynamic_index_in_dim(owners, core, 1, keepdims=False)
    theirs = swap_core(lax.dynamic_index_in_dim(owners, 1 - core, 1, keepdims=False))
    partial = project(y[None].astype(jnp.int32), mine, theirs, w_out, w_sib)
    parts = [partial[0]] + [along_y(partial[d], d) for d in (1, 2, 3)]
    hidden, send_in = norm_dispatch(x_resid, parts, gain, target_rows, slots)
    recv_in = exchange(send_in).reshape(slots, width)
    both = experts(recv_in, *down_part(where, recv_grad, downs, runs), chunk)
    rows = exchange(both).reshape(sources * BACK, width)
    return combine(hidden, grad_out, rows, returned, gate_prob, gain)


def solution(mesh):
    tokens = P(("seq", "exp"), None)
    heads = P("seq", "exp")
    placed = (
        tokens,
        heads,
        heads,
        heads,
        P("exp", None),
        P(),
        P("exp", "seq", None),
        P("exp", "seq", None),
        P("exp", None, "seq"),
        tokens,
        tokens,
        tokens,
    )
    return jax.shard_map(
        per_device, mesh=mesh, in_specs=placed, out_specs=(tokens, tokens, tokens), check_vma=False
    )
```

```python
import functools
import math

import jax
import jax.numpy as jnp
from jax import lax
from jax.experimental import pallas as pl
from jax.experimental.pallas import tpu as pltpu
from jax.sharding import PartitionSpec as P

HD = 128
W = 2048
CAP = 18
SLOT = 24
BACK = 40
NZ = 8
NX = 4
NY = 4
norm_eps = 1e-06
F32 = jnp.float32
BF16 = jnp.bfloat16
VMEM = pl.BlockSpec(memory_space=pltpu.VMEM)
SMEM = pl.BlockSpec(memory_space=pltpu.SMEM)
HBM = pl.BlockSpec(memory_space=pltpu.HBM)


def params(mib):
    return pltpu.CompilerParams(vmem_limit_bytes=mib * 2**20)


def nt(a, b):
    return lax.dot_general(a, b, (((1,), (1,)), ((), ())), preferred_element_type=F32)


def nn(a, b):
    return jnp.dot(a, b, preferred_element_type=F32)


def shift_zx(block, dz, dx):
    route = [(s, ((s // NX + dz) % NZ) * NX + (s % NX + dx) % NX) for s in range(NZ * NX)]
    return lax.ppermute(block, "seq", route)


def along_z(block, d):
    return shift_zx(block, d, 0)


def along_x(block, d):
    return shift_zx(block, 0, d)


def along_y(block, d):
    return lax.ppermute(block, "exp", [(i, (i + 2 * d) % (2 * NY)) for i in range(2 * NY)])


def swap_core(block):
    return lax.ppermute(block, "exp", [(i, i ^ 1) for i in range(2 * NY)])


def after(value, *earlier):
    return lax.optimization_barrier((value, earlier))[0]


def opposite(ahead, behind, cut, move):
    return [move(ahead[:cut], 1), move(behind[cut:], -1)]


def to_earlier(own):
    x = lax.axis_index("seq") % NX
    above = along_z(own, 1)
    return above, (
        jnp.where(x == NX - 1, above, own),
        jnp.where(x < 2, own, above),
        jnp.where(x == 0, own, above),
    )


def earlier_shards(above, loads):
    return [along_x(loads[0], 1), along_x(loads[1], 2), along_x(loads[2], -1), above]


def attention_kernel(where, q, *refs):
    both, out = refs[:-1], refs[-1]
    rows, span = 128, both[0].shape[0] // 2
    scale = 1.0 / math.sqrt(HD)
    seq = where[0]

    def block(i, _):
        at = pl.multiple_of(i * rows, rows)
        qpos = at + lax.broadcasted_iota(jnp.int32, (rows, span), 0)
        kpos = lax.broadcasted_iota(jnp.int32, (rows, span), 1)
        for h in range(out.shape[1] // HD):
            cols = slice(h * HD, (h + 1) * HD)
            queries = q[pl.ds(at, rows), cols]
            scores = []
            for d in range(5):
                s = nt(queries, both[d][:span, cols]) * scale
                if d == 0:
                    s = jnp.where(kpos <= qpos, s, -jnp.inf)
                elif d == 4:
                    s = jnp.where((kpos > qpos) & (seq >= d), s, -jnp.inf)
                else:
                    s = jnp.where(seq >= d, s, -jnp.inf)
                scores.append(s)
            top = scores[0]
            for s in scores[1:]:
                top = jnp.maximum(top, s)
            top = jnp.max(top, axis=-1, keepdims=True)
            mixed = jnp.zeros((rows, HD), F32)
            total = jnp.zeros((rows, span), F32)
            for d in range(5):
                e = jnp.exp(scores[d] - top)
                total = total + e
                mixed = mixed + nn(e.astype(BF16), both[d][span:, cols])
            out[pl.ds(at, rows), cols] = (mixed / jnp.sum(total, axis=-1, keepdims=True)).astype(BF16)
        return 0

    lax.fori_loop(0, q.shape[0] // rows, block, 0)


def attention(where, q, both):
    return pl.pallas_call(
        attention_kernel,
        out_shape=jax.ShapeDtypeStruct(q.shape, BF16),
        in_specs=[SMEM] + [VMEM] * (1 + len(both)),
        out_specs=VMEM,
        compiler_params=params(24),
        cost_estimate=pl.CostEstimate(flops=4 * 512 * 2560 * 256, bytes_accessed=6 * 2**20, transcendentals=512 * 2560 * 2),
    )(where, q, *both)


def round_z(block, cut, first=None):
    ahead, behind = [along_z(block, 1)], [along_z(block, -1)]
    for i in range(2):
        a, b = ahead[-1], behind[-1]
        if i == 0 and first is not None:
            a, b = after(a, first), after(b, first)
        ahead.append(along_z(a, 1))
        behind.append(along_z(b, -1))
    return ahead, behind, opposite(ahead[2], behind[2], cut, along_z)


def gather_rows(rows, above, arrived):
    half = rows.shape[0] // 2
    a, b = rows[:half], rows[half:]
    plane = jnp.concatenate([a, along_x(a, 1), along_x(a, 2), along_x(a, -1)], axis=0)
    up, down, far = round_z(b, half // 2, above)
    column = jnp.concatenate([b] + up + down + far, axis=0)
    depths = (0, 1, 2, 3, 7, 6, 5, 4)
    plane = after(plane, far)
    ahead, behind, far = round_z(plane, NX // 2 * half)
    pieces = [(plane, 0)]
    for i in range(3):
        pieces += [(ahead[i], i + 1), (behind[i], NZ - 1 - i)]
    listed = [[(dx * half, 0, half, dz, dx) for dx in range(NX)] for _, dz in pieces]
    listed += [[(dx % 2 * half, 0, half, NZ // 2, dx) for dx in pair] for pair in ((0, 1), (2, 3))]
    pieces = [p for p, _ in pieces] + far
    sent = after(column, arrived)
    pieces += [column] + [along_x(sent, d) for d in (1, 2, -1)]
    listed += [[(i * half, half, half, dz, dx) for i, dz in enumerate(depths)] for dx in range(NX)]
    return pieces, listed


def project_kernel(where, own, sib, w_own, w_sib, out):
    for d in range(NY):
        y = lax.rem(where[0] + d, NY)
        out[d] = (nn(own[y], w_own[...]) + nn(sib[y], w_sib[...])).astype(BF16)


def project(where, own, sib, w_own, w_sib):
    return pl.pallas_call(
        project_kernel,
        out_shape=jax.ShapeDtypeStruct((NY, own.shape[1], w_own.shape[1]), BF16),
        in_specs=[pl.BlockSpec(memory_space=pltpu.SMEM)] + [VMEM] * 4,
        out_specs=VMEM,
        compiler_params=params(24),
        cost_estimate=pl.CostEstimate(flops=2 * 256 * 512 * 2048, bytes_accessed=6 * 2**20, transcendentals=0),
    )(where, own, sib, w_own, w_sib)


def slots_of(target_rows, slots, tokens):
    at = lax.broadcasted_iota(jnp.int32, (slots, tokens), 0)
    hit = (at == target_rows[0:1, :]) | (at == target_rows[1:2, :])
    return jnp.where(hit, 1.0, 0.0).astype(BF16)


def norm_kernel(x, p0, p1, p2, p3, gain, target_rows, hidden, send):
    total = p0[...].astype(F32) + p1[...].astype(F32) + p2[...].astype(F32) + p3[...].astype(F32)
    state = (x[...].astype(F32) + total).astype(BF16)
    hidden[...] = state
    wide = state.astype(F32)
    rstd = lax.rsqrt(jnp.mean(wide * wide, axis=-1, keepdims=True) + norm_eps)
    moe_in = (wide * rstd * gain[...]).astype(BF16)
    place = slots_of(target_rows, send.shape[0], x.shape[0])
    send[...] = nn(place, moe_in).astype(BF16)


def norm_dispatch(x, parts, gain, target_rows, slots):
    tokens, width = x.shape
    return pl.pallas_call(
        norm_kernel,
        out_shape=(
            jax.ShapeDtypeStruct((tokens, width), BF16),
            jax.ShapeDtypeStruct((slots, width), BF16),
        ),
        in_specs=[VMEM] * 7,
        out_specs=(VMEM, VMEM),
        compiler_params=params(24),
        cost_estimate=pl.CostEstimate(flops=2 * slots * tokens * width, bytes_accessed=3 * 2**20, transcendentals=0),
    )(x, *parts, gain, target_rows)


def scatter_kernel(rows, target_rows, send):
    place = slots_of(target_rows, send.shape[0], rows.shape[0])
    send[...] = nn(place, rows[...]).astype(BF16)


def scatter_rows(rows, target_rows, slots):
    return pl.pallas_call(
        scatter_kernel,
        out_shape=jax.ShapeDtypeStruct((slots, rows.shape[1]), BF16),
        in_specs=[VMEM] * 2,
        out_specs=VMEM,
        compiler_params=params(16),
        cost_estimate=pl.CostEstimate(flops=2 * slots * 64 * 2048, bytes_accessed=2**20, transcendentals=0),
    )(rows, target_rows)


def fetch_rows(runs, seq, pieces, wd, sem):
    z, x = seq // NX, lax.rem(seq, NX)
    part = wd.shape[0] // (NZ * NX)
    for piece, listed in zip(pieces, runs):
        for first, offset, count, dz, dx in listed:
            source = lax.rem(z + NZ - dz, NZ) * NX + lax.rem(x + NX - dx, NX)
            row = pl.multiple_of(source * part + offset, count)
            pltpu.make_async_copy(piece.at[pl.ds(first, count)], wd.at[pl.ds(row, count)], sem).start()


def down_kernel(runs, where, rows_grad, *refs):
    pieces, (back, wd, sem) = refs[: len(runs)], refs[len(runs) :]
    fetch_rows(runs, where[0], pieces, wd, sem)
    pltpu.make_async_copy(wd, wd, sem).wait()
    span = 256
    for k in range(wd.shape[0] // span):
        cols = pl.ds(k * span, span)
        term = nn(rows_grad[:, cols], wd[cols, :])
        back[...] = term if k == 0 else back[...] + term


def down_part(where, rows_grad, pieces, runs):
    rows, width = rows_grad.shape
    hidden = pieces[0].shape[1]
    return pl.pallas_call(
        functools.partial(down_kernel, runs),
        out_shape=jax.ShapeDtypeStruct((rows, hidden), F32),
        in_specs=[SMEM, VMEM] + [HBM] * len(pieces),
        out_specs=VMEM,
        scratch_shapes=[pltpu.VMEM((width, hidden), BF16), pltpu.SemaphoreType.DMA(())],
        compiler_params=params(16),
        cost_estimate=pl.CostEstimate(flops=2 * rows * width * hidden, bytes_accessed=7 * 2**20, transcendentals=0),
    )(where, rows_grad, *pieces)


def expert_kernel(runs, where, rows_in, ba, chunk, *refs):
    pieces, (both, wg, wu, wd, ga, ua, hid, gpg, gpu, sems, down_sem) = refs[: len(runs)], refs[len(runs) :]
    shards = chunk.shape[0]
    part = chunk.shape[1] // 2
    mats = (wg, wu)
    group = 4
    steps = shards // group
    span = group * part

    def start(s, _):
        row = pl.multiple_of(s * part, part)
        for m in range(2):
            pltpu.make_async_copy(
                chunk.at[s, pl.ds(m * part, part)], mats[m].at[pl.ds(row, part)], sems.at[m, s // group]
            ).start()
        return 0

    lax.fori_loop(0, shards, start, 0)
    fetch_rows(runs, where[0], pieces, wd, down_sem)
    for k in range(steps):
        cols = pl.ds(k * span, span)
        for m, acc in ((0, ga), (1, ua)):
            view = mats[m].at[cols]
            pltpu.make_async_copy(view, view, sems.at[m, k]).wait()
            term = nn(rows_in[:, cols], mats[m][cols, :])
            acc[...] = term if k == 0 else acc[...] + term

    def point(i, _):
        r = pl.ds(pl.multiple_of(i * 16, 16), 16)
        gate, up, grad = ga[r, :], ua[r, :], ba[r, :]
        sigma = jax.nn.sigmoid(gate)
        act = gate * sigma
        hid[r, :] = (act * up).astype(BF16)
        gpg[r, :] = (grad * up * sigma * (1.0 + gate * (1.0 - sigma))).astype(BF16)
        gpu[r, :] = (grad * act).astype(BF16)
        return 0

    lax.fori_loop(0, hid.shape[0] // 16, point, 0)
    pltpu.make_async_copy(wd, wd, down_sem).wait()
    sources = 2 * NY

    def finish(k, _):
        cols = pl.ds(pl.multiple_of(k * span, span), span)
        out = nt(hid[...], wd[cols, :]).reshape(sources, SLOT, span)
        back = (nt(gpg[...], wg[cols, :]) + nt(gpu[...], wu[cols, :])).reshape(sources, SLOT, span)
        rest = jnp.zeros((sources, BACK - 2 * CAP, span), F32)
        joined = jnp.concatenate([out[:, :CAP], back[:, :CAP], rest], axis=1)
        both[:, cols] = joined.reshape(sources * BACK, span).astype(BF16)
        return 0

    lax.fori_loop(0, steps, finish, 0)


def experts(where, rows_in, back, chunk, pieces, runs):
    rows, width = rows_in.shape
    shards, hidden = chunk.shape[0], chunk.shape[2]
    return pl.pallas_call(
        functools.partial(expert_kernel, runs),
        out_shape=jax.ShapeDtypeStruct((2 * NY * BACK, width), BF16),
        in_specs=[SMEM, VMEM, VMEM, HBM] + [HBM] * len(pieces),
        out_specs=VMEM,
        scratch_shapes=[pltpu.VMEM((width, hidden), BF16)] * 3
        + [pltpu.VMEM((rows, hidden), F32)] * 2
        + [pltpu.VMEM((rows, hidden), BF16)] * 3
        + [pltpu.SemaphoreType.DMA((2, shards // 4)), pltpu.SemaphoreType.DMA(())],
        compiler_params=params(47),
        cost_estimate=pl.CostEstimate(
            flops=10 * rows * width * hidden, bytes_accessed=14 * 2**20, transcendentals=rows * hidden
        ),
    )(where, rows_in, back, chunk, *pieces)


def combine_kernel(hidden, grad_out, rows, target, prob, gain, layer_out, grad_in, grad_gate):
    tokens = hidden.shape[0]
    at = lax.broadcasted_iota(jnp.int32, (tokens, rows.shape[0]), 1)

    def picked(c, offset):
        place = jnp.where(at == target[:, c : c + 1] + offset, 1.0, 0.0).astype(BF16)
        return nn(place, rows[...])

    wide = hidden[...].astype(F32)
    grad = grad_out[...].astype(F32)
    out0, out1 = picked(0, 0), picked(1, 0)
    p0, p1 = prob[:, 0:1], prob[:, 1:2]
    layer_out[...] = (wide + (p0 * out0 + p1 * out1)).astype(BF16)
    grad_gate[:, 0:1] = jnp.sum(grad * out0, axis=-1, keepdims=True)
    grad_gate[:, 1:2] = jnp.sum(grad * out1, axis=-1, keepdims=True)
    moe_grad = p0 * picked(0, CAP) + p1 * picked(1, CAP)
    rstd = lax.rsqrt(jnp.mean(wide * wide, axis=-1, keepdims=True) + norm_eps)
    normed = wide * rstd
    scaled = moe_grad * gain[...]
    mean = jnp.mean(scaled * normed, axis=-1, keepdims=True)
    grad_in[...] = (grad + rstd * (scaled - normed * mean)).astype(BF16)


def combine(hidden, grad_out, rows, target, prob, gain):
    tokens, width = hidden.shape
    made = jax.ShapeDtypeStruct((tokens, width), BF16)
    return pl.pallas_call(
        combine_kernel,
        out_shape=(made, made, jax.ShapeDtypeStruct((tokens, 2), F32)),
        in_specs=[VMEM] * 6,
        out_specs=(VMEM,) * 3,
        compiler_params=params(24),
        cost_estimate=pl.CostEstimate(flops=2**28, bytes_accessed=3 * 2**20, transcendentals=0),
    )(hidden, grad_out, rows, target, prob, gain)


def per_device(
    x_resid, queries, key_proj, val_proj, w_out, norm_gain, w_gate, w_up, w_down, routes, gate_prob, grad_out
):
    tok_dev, width = x_resid.shape
    me_seq, me_exp = lax.axis_index("seq"), lax.axis_index("exp")
    where = jnp.stack([me_seq, me_exp // 2, me_exp % 2]).astype(jnp.int32)
    core, y = me_exp % 2, me_exp // 2
    chunk = lax.all_gather(jnp.concatenate([w_gate[0], w_up[0]], axis=0), "seq", axis=0)
    own = jnp.concatenate([key_proj, val_proj], axis=0)
    above, loads = to_earlier(own)
    both = [own] + earlier_shards(above, loads)
    downs, runs = gather_rows(w_down[0].T, above, both)
    w_sib = swap_core(after(w_out, above))

    flat = routes.reshape(-1)
    order = jnp.arange(flat.shape[0], dtype=jnp.int32)
    same = (flat[:, None] == flat[None, :]) & (order[None, :] < order[:, None])
    rank = jnp.sum(same.astype(jnp.int32), axis=1)
    target_rows = (flat * SLOT + rank).reshape(tok_dev, 2).T
    returned = (flat * BACK + rank).reshape(tok_dev, 2)
    sources = 2 * NY
    slots = sources * SLOT
    gain = norm_gain[None, :]

    def exchange(rows):
        split = rows.reshape(sources, rows.shape[0] // sources, rows.shape[1])
        return lax.all_to_all(split, "exp", split_axis=0, concat_axis=0, tiled=True)

    recv_grad = exchange(scatter_rows(after(grad_out, both), target_rows, slots)).reshape(slots, width)
    attn = attention(where, queries, both)
    owners = attn.reshape(NY, 2, tok_dev, attn.shape[1])
    mine = lax.dynamic_index_in_dim(owners, core, 1, keepdims=False)
    theirs = swap_core(lax.dynamic_index_in_dim(owners, 1 - core, 1, keepdims=False))
    partial = project(y[None].astype(jnp.int32), mine, theirs, w_out, w_sib)
    sent = after(partial, *downs[-3:])
    parts = [partial[0]] + [along_y(sent[d], d) for d in (1, 2, 3)]
    hidden, send_in = norm_dispatch(x_resid, parts, gain, target_rows, slots)
    recv_in = exchange(send_in).reshape(slots, width)
    back = down_part(where, recv_grad, downs, runs)
    results = experts(where, recv_in, back, chunk, downs, runs)
    rows = exchange(results).reshape(sources * BACK, width)
    return combine(hidden, grad_out, rows, returned, gate_prob, gain)


def solution(mesh):
    tokens = P(("seq", "exp"), None)
    heads = P("seq", "exp")
    placed = (
        tokens,
        heads,
        heads,
        heads,
        P("exp", None),
        P(),
        P("exp", "seq", None),
        P("exp", "seq", None),
        P("exp", None, "seq"),
        tokens,
        tokens,
        tokens,
    )
    return jax.shard_map(
        per_device, mesh=mesh, in_specs=placed, out_specs=(tokens, tokens, tokens), check_vma=False
    )
```

```python
import functools
import math

import jax
import jax.numpy as jnp
from jax import lax
from jax.experimental import pallas as pl
from jax.experimental.pallas import tpu as pltpu
from jax.sharding import PartitionSpec as P

HD = 128
W = 2048
CAP = 18
SLOT = 24
BACK = 40
NZ = 8
NX = 4
NY = 4
norm_eps = 1e-06
F32 = jnp.float32
BF16 = jnp.bfloat16
VMEM = pl.BlockSpec(memory_space=pltpu.VMEM)
SMEM = pl.BlockSpec(memory_space=pltpu.SMEM)
HBM = pl.BlockSpec(memory_space=pltpu.HBM)


def params(mib):
    return pltpu.CompilerParams(vmem_limit_bytes=mib * 2**20)


def nt(a, b):
    return lax.dot_general(a, b, (((1,), (1,)), ((), ())), preferred_element_type=F32)


def nn(a, b):
    return jnp.dot(a, b, preferred_element_type=F32)


def shift_zx(block, dz, dx):
    route = [(s, ((s // NX + dz) % NZ) * NX + (s % NX + dx) % NX) for s in range(NZ * NX)]
    return lax.ppermute(block, "seq", route)


def along_z(block, d):
    return shift_zx(block, d, 0)


def along_x(block, d):
    return shift_zx(block, 0, d)


def along_y(block, d):
    return lax.ppermute(block, "exp", [(i, (i + 2 * d) % (2 * NY)) for i in range(2 * NY)])


def swap_core(block):
    return lax.ppermute(block, "exp", [(i, i ^ 1) for i in range(2 * NY)])


def after(value, *earlier):
    return lax.optimization_barrier((value, earlier))[0]


def opposite(ahead, behind, cut, move):
    return [move(ahead[:cut], 1), move(behind[cut:], -1)]


def to_earlier(own):
    x = lax.axis_index("seq") % NX
    above = along_z(own, 1)
    return above, (
        jnp.where(x == NX - 1, above, own),
        jnp.where(x < 2, own, above),
        jnp.where(x == 0, own, above),
    )


def earlier_shards(above, loads):
    return [along_x(loads[0], 1), along_x(loads[1], 2), along_x(loads[2], -1), above]


def attention_kernel(where, q, k0, k1, k2, k3, k4, v0, v1, v2, v3, v4, out):
    keys, vals = (k0, k1, k2, k3, k4), (v0, v1, v2, v3, v4)
    rows, span = 128, k0.shape[0]
    scale = 1.0 / math.sqrt(HD)
    seq = where[0]

    def block(i, _):
        at = pl.multiple_of(i * rows, rows)
        qpos = at + lax.broadcasted_iota(jnp.int32, (rows, span), 0)
        kpos = lax.broadcasted_iota(jnp.int32, (rows, span), 1)
        for h in range(out.shape[1] // HD):
            cols = slice(h * HD, (h + 1) * HD)
            queries = q[pl.ds(at, rows), cols]
            scores = []
            for d in range(5):
                s = nt(queries, keys[d][:, cols]) * scale
                if d == 0:
                    s = jnp.where(kpos <= qpos, s, -jnp.inf)
                elif d == 4:
                    s = jnp.where((kpos > qpos) & (seq >= d), s, -jnp.inf)
                else:
                    s = jnp.where(seq >= d, s, -jnp.inf)
                scores.append(s)
            top = scores[0]
            for s in scores[1:]:
                top = jnp.maximum(top, s)
            top = jnp.max(top, axis=-1, keepdims=True)
            mixed = jnp.zeros((rows, HD), F32)
            total = jnp.zeros((rows, span), F32)
            for d in range(5):
                e = jnp.exp(scores[d] - top)
                total = total + e
                mixed = mixed + nn(e.astype(BF16), vals[d][:, cols])
            out[pl.ds(at, rows), cols] = (mixed / jnp.sum(total, axis=-1, keepdims=True)).astype(BF16)
        return 0

    lax.fori_loop(0, q.shape[0] // rows, block, 0)


def attention(where, q, keys, vals):
    return pl.pallas_call(
        attention_kernel,
        out_shape=jax.ShapeDtypeStruct(q.shape, BF16),
        in_specs=[SMEM] + [VMEM] * 11,
        out_specs=VMEM,
        compiler_params=params(24),
        cost_estimate=pl.CostEstimate(flops=4 * 512 * 2560 * 256, bytes_accessed=6 * 2**20, transcendentals=512 * 2560 * 2),
    )(where, q, *keys, *vals)


def round_z(block, cut, first=None):
    ahead, behind = [along_z(block, 1)], [along_z(block, -1)]
    for i in range(2):
        a, b = ahead[-1], behind[-1]
        if i == 0 and first is not None:
            a, b = after(a, first), after(b, first)
        ahead.append(along_z(a, 1))
        behind.append(along_z(b, -1))
    return ahead, behind, opposite(ahead[2], behind[2], cut, along_z)


def gather_rows(rows, above, arrived):
    half = rows.shape[0] // 2
    a, b = rows[:half], rows[half:]
    plane = jnp.concatenate([a, along_x(a, 1), along_x(a, 2), along_x(a, -1)], axis=0)
    up, down, far = round_z(b, half // 2, above)
    column = jnp.concatenate([b] + up + down + far, axis=0)
    depths = (0, 1, 2, 3, 7, 6, 5, 4)
    plane = after(plane, up[2], down[2])
    ahead, behind, far = round_z(plane, NX // 2 * half)
    pieces = [(plane, 0)]
    for i in range(3):
        pieces += [(ahead[i], i + 1), (behind[i], NZ - 1 - i)]
    listed = [[(dx * half, 0, half, dz, dx) for dx in range(NX)] for _, dz in pieces]
    listed += [[(dx % 2 * half, 0, half, NZ // 2, dx) for dx in pair] for pair in ((0, 1), (2, 3))]
    pieces = [p for p, _ in pieces] + far
    sent = after(column, arrived)
    pieces += [column] + [along_x(sent, d) for d in (1, 2, -1)]
    listed += [[(i * half, half, half, dz, dx) for i, dz in enumerate(depths)] for dx in range(NX)]
    return pieces, listed


def project_kernel(where, own, sib, w_own, w_sib, out):
    for d in range(NY):
        y = lax.rem(where[0] + d, NY)
        out[d] = (nn(own[y], w_own[...]) + nn(sib[y], w_sib[...])).astype(BF16)


def project(where, own, sib, w_own, w_sib):
    return pl.pallas_call(
        project_kernel,
        out_shape=jax.ShapeDtypeStruct((NY, own.shape[1], w_own.shape[1]), BF16),
        in_specs=[pl.BlockSpec(memory_space=pltpu.SMEM)] + [VMEM] * 4,
        out_specs=VMEM,
        compiler_params=params(24),
        cost_estimate=pl.CostEstimate(flops=2 * 256 * 512 * 2048, bytes_accessed=6 * 2**20, transcendentals=0),
    )(where, own, sib, w_own, w_sib)


def slots_of(target_rows, slots, tokens):
    at = lax.broadcasted_iota(jnp.int32, (slots, tokens), 0)
    hit = (at == target_rows[0:1, :]) | (at == target_rows[1:2, :])
    return jnp.where(hit, 1.0, 0.0).astype(BF16)


def norm_kernel(x, p0, p1, p2, p3, gain, target_rows, hidden, send):
    total = p0[...].astype(F32) + p1[...].astype(F32) + p2[...].astype(F32) + p3[...].astype(F32)
    state = (x[...].astype(F32) + total).astype(BF16)
    hidden[...] = state
    wide = state.astype(F32)
    rstd = lax.rsqrt(jnp.mean(wide * wide, axis=-1, keepdims=True) + norm_eps)
    moe_in = (wide * rstd * gain[...]).astype(BF16)
    place = slots_of(target_rows, send.shape[0], x.shape[0])
    send[...] = nn(place, moe_in).astype(BF16)


def norm_dispatch(x, parts, gain, target_rows, slots):
    tokens, width = x.shape
    return pl.pallas_call(
        norm_kernel,
        out_shape=(
            jax.ShapeDtypeStruct((tokens, width), BF16),
            jax.ShapeDtypeStruct((slots, width), BF16),
        ),
        in_specs=[VMEM] * 7,
        out_specs=(VMEM, VMEM),
        compiler_params=params(24),
        cost_estimate=pl.CostEstimate(flops=2 * slots * tokens * width, bytes_accessed=3 * 2**20, transcendentals=0),
    )(x, *parts, gain, target_rows)


def scatter_kernel(rows, target_rows, send):
    place = slots_of(target_rows, send.shape[0], rows.shape[0])
    send[...] = nn(place, rows[...]).astype(BF16)


def scatter_rows(rows, target_rows, slots):
    return pl.pallas_call(
        scatter_kernel,
        out_shape=jax.ShapeDtypeStruct((slots, rows.shape[1]), BF16),
        in_specs=[VMEM] * 2,
        out_specs=VMEM,
        compiler_params=params(16),
        cost_estimate=pl.CostEstimate(flops=2 * slots * 64 * 2048, bytes_accessed=2**20, transcendentals=0),
    )(rows, target_rows)


def fetch_rows(runs, seq, pieces, wd, sem):
    z, x = seq // NX, lax.rem(seq, NX)
    part = wd.shape[0] // (NZ * NX)
    for piece, listed in zip(pieces, runs):
        for first, offset, count, dz, dx in listed:
            source = lax.rem(z + NZ - dz, NZ) * NX + lax.rem(x + NX - dx, NX)
            row = pl.multiple_of(source * part + offset, count)
            pltpu.make_async_copy(piece.at[pl.ds(first, count)], wd.at[pl.ds(row, count)], sem).start()


def expert_kernel(runs, where, rows_in, rows_grad, chunk, *refs):
    pieces, (both, wg, wu, wd, ga, ua, ba, hid, gpg, gpu, sems, down_sem) = refs[: len(runs)], refs[len(runs) :]
    shards = chunk.shape[0]
    part = chunk.shape[1] // 2
    mats = (wg, wu)
    group = 4
    steps = shards // group
    span = group * part

    def start(s, _):
        row = pl.multiple_of(s * part, part)
        for m in range(2):
            pltpu.make_async_copy(
                chunk.at[s, pl.ds(m * part, part)], mats[m].at[pl.ds(row, part)], sems.at[m, s // group]
            ).start()
        return 0

    lax.fori_loop(0, shards, start, 0)
    fetch_rows(runs, where[0], pieces, wd, down_sem)
    for k in range(steps):
        cols = pl.ds(k * span, span)
        for m, acc in ((0, ga), (1, ua)):
            view = mats[m].at[cols]
            pltpu.make_async_copy(view, view, sems.at[m, k]).wait()
            term = nn(rows_in[:, cols], mats[m][cols, :])
            acc[...] = term if k == 0 else acc[...] + term
    pltpu.make_async_copy(wd, wd, down_sem).wait()
    for k in range(steps):
        cols = pl.ds(k * span, span)
        term = nn(rows_grad[:, cols], wd[cols, :])
        ba[...] = term if k == 0 else ba[...] + term

    def point(i, _):
        r = pl.ds(pl.multiple_of(i * 16, 16), 16)
        gate, up, grad = ga[r, :], ua[r, :], ba[r, :]
        sigma = jax.nn.sigmoid(gate)
        act = gate * sigma
        hid[r, :] = (act * up).astype(BF16)
        gpg[r, :] = (grad * up * sigma * (1.0 + gate * (1.0 - sigma))).astype(BF16)
        gpu[r, :] = (grad * act).astype(BF16)
        return 0

    lax.fori_loop(0, hid.shape[0] // 16, point, 0)
    sources = 2 * NY

    def finish(k, _):
        cols = pl.ds(pl.multiple_of(k * span, span), span)
        out = nt(hid[...], wd[cols, :]).reshape(sources, SLOT, span)
        back = (nt(gpg[...], wg[cols, :]) + nt(gpu[...], wu[cols, :])).reshape(sources, SLOT, span)
        rest = jnp.zeros((sources, BACK - 2 * CAP, span), F32)
        joined = jnp.concatenate([out[:, :CAP], back[:, :CAP], rest], axis=1)
        both[:, cols] = joined.reshape(sources * BACK, span).astype(BF16)
        return 0

    lax.fori_loop(0, steps, finish, 0)


def experts(where, rows_in, rows_grad, chunk, pieces, runs):
    rows, width = rows_in.shape
    shards, hidden = chunk.shape[0], chunk.shape[2]
    return pl.pallas_call(
        functools.partial(expert_kernel, runs),
        out_shape=jax.ShapeDtypeStruct((2 * NY * BACK, width), BF16),
        in_specs=[SMEM, VMEM, VMEM, HBM] + [HBM] * len(pieces),
        out_specs=VMEM,
        scratch_shapes=[pltpu.VMEM((width, hidden), BF16)] * 3
        + [pltpu.VMEM((rows, hidden), F32)] * 3
        + [pltpu.VMEM((rows, hidden), BF16)] * 3
        + [pltpu.SemaphoreType.DMA((2, shards // 4)), pltpu.SemaphoreType.DMA(())],
        compiler_params=params(47),
        cost_estimate=pl.CostEstimate(
            flops=12 * rows * width * hidden, bytes_accessed=20 * 2**20, transcendentals=rows * hidden
        ),
    )(where, rows_in, rows_grad, chunk, *pieces)


def combine_kernel(hidden, grad_out, rows, target, prob, gain, layer_out, grad_in, grad_gate):
    tokens = hidden.shape[0]
    at = lax.broadcasted_iota(jnp.int32, (tokens, rows.shape[0]), 1)

    def picked(c, offset):
        place = jnp.where(at == target[:, c : c + 1] + offset, 1.0, 0.0).astype(BF16)
        return nn(place, rows[...])

    wide = hidden[...].astype(F32)
    grad = grad_out[...].astype(F32)
    out0, out1 = picked(0, 0), picked(1, 0)
    p0, p1 = prob[:, 0:1], prob[:, 1:2]
    layer_out[...] = (wide + (p0 * out0 + p1 * out1)).astype(BF16)
    grad_gate[:, 0:1] = jnp.sum(grad * out0, axis=-1, keepdims=True)
    grad_gate[:, 1:2] = jnp.sum(grad * out1, axis=-1, keepdims=True)
    moe_grad = p0 * picked(0, CAP) + p1 * picked(1, CAP)
    rstd = lax.rsqrt(jnp.mean(wide * wide, axis=-1, keepdims=True) + norm_eps)
    normed = wide * rstd
    scaled = moe_grad * gain[...]
    mean = jnp.mean(scaled * normed, axis=-1, keepdims=True)
    grad_in[...] = (grad + rstd * (scaled - normed * mean)).astype(BF16)


def combine(hidden, grad_out, rows, target, prob, gain):
    tokens, width = hidden.shape
    made = jax.ShapeDtypeStruct((tokens, width), BF16)
    return pl.pallas_call(
        combine_kernel,
        out_shape=(made, made, jax.ShapeDtypeStruct((tokens, 2), F32)),
        in_specs=[VMEM] * 6,
        out_specs=(VMEM,) * 3,
        compiler_params=params(24),
        cost_estimate=pl.CostEstimate(flops=2**28, bytes_accessed=3 * 2**20, transcendentals=0),
    )(hidden, grad_out, rows, target, prob, gain)


def per_device(
    x_resid, queries, key_proj, val_proj, w_out, norm_gain, w_gate, w_up, w_down, routes, gate_prob, grad_out
):
    tok_dev, width = x_resid.shape
    me_seq, me_exp = lax.axis_index("seq"), lax.axis_index("exp")
    where = jnp.stack([me_seq, me_exp // 2, me_exp % 2]).astype(jnp.int32)
    core, y = me_exp % 2, me_exp // 2
    chunk = lax.all_gather(jnp.concatenate([w_gate[0], w_up[0]], axis=0), "seq", axis=0)
    (k_above, k_loads), (v_above, v_loads) = to_earlier(key_proj), to_earlier(val_proj)
    keys = [key_proj] + earlier_shards(k_above, k_loads)
    vals = [val_proj] + earlier_shards(v_above, v_loads)
    downs, runs = gather_rows(w_down[0].T, k_above, (keys, vals))
    w_sib = swap_core(after(w_out, keys))

    flat = routes.reshape(-1)
    order = jnp.arange(flat.shape[0], dtype=jnp.int32)
    same = (flat[:, None] == flat[None, :]) & (order[None, :] < order[:, None])
    rank = jnp.sum(same.astype(jnp.int32), axis=1)
    target_rows = (flat * SLOT + rank).reshape(tok_dev, 2).T
    returned = (flat * BACK + rank).reshape(tok_dev, 2)
    sources = 2 * NY
    slots = sources * SLOT
    gain = norm_gain[None, :]

    def exchange(rows):
        split = rows.reshape(sources, rows.shape[0] // sources, rows.shape[1])
        return lax.all_to_all(split, "exp", split_axis=0, concat_axis=0, tiled=True)

    recv_grad = exchange(scatter_rows(after(grad_out, keys), target_rows, slots)).reshape(slots, width)
    attn = attention(where, queries, keys, vals)
    owners = attn.reshape(NY, 2, tok_dev, attn.shape[1])
    mine = lax.dynamic_index_in_dim(owners, core, 1, keepdims=False)
    theirs = swap_core(lax.dynamic_index_in_dim(owners, 1 - core, 1, keepdims=False))
    partial = project(y[None].astype(jnp.int32), mine, theirs, w_out, w_sib)
    parts = [partial[0]] + [along_y(partial[d], d) for d in (1, 2, 3)]
    hidden, send_in = norm_dispatch(x_resid, parts, gain, target_rows, slots)
    recv_in = exchange(send_in).reshape(slots, width)
    both = experts(where, recv_in, recv_grad, chunk, downs, runs)
    rows = exchange(both).reshape(sources * BACK, width)
    return combine(hidden, grad_out, rows, returned, gate_prob, gain)


def solution(mesh):
    tokens = P(("seq", "exp"), None)
    heads = P("seq", "exp")
    placed = (
        tokens,
        heads,
        heads,
        heads,
        P("exp", None),
        P(),
        P("exp", "seq", None),
        P("exp", "seq", None),
        P("exp", None, "seq"),
        tokens,
        tokens,
        tokens,
    )
    return jax.shard_map(
        per_device, mesh=mesh, in_specs=placed, out_specs=(tokens, tokens, tokens), check_vma=False
    )
```
